128 devices in a mesh: dp: 16 (over x_hi, z, core), mp: 8 (over y, x_lo).
Axes of the slice: x: 4 (x_hi: 2, x_lo: 2; x = x_hi * 2 + x_lo), y: 4, z: 4, core: 2. Of those that a mesh axis runs over, the one named last changes fastest.
Arguments:
- hidden: bfloat16 [32, 1024, 1536], P('dp', 'mp'), may hold values from -6 to 6
- segments: int32 [32, 1024], P('dp'), may hold values from 0 to 4, as said below
- cotangent: bfloat16 [32, 1024, 1536], P('dp', 'mp'), may hold values from -6 to 6
- norm_gain: bfloat16 [1536], P(('dp', 'mp')), may hold values from 0.5 to 1.5
- w_z: bfloat16 [1536, 3072], P('dp', 'mp'), may hold values from -0.15625 to 0.15625
- w_x: bfloat16 [1536, 3072], P('dp', 'mp'), may hold values from -0.15625 to 0.15625
- w_dt: bfloat16 [1536, 48], P('dp', 'mp'), may hold values from -0.15625 to 0.15625
- w_bc: bfloat16 [1536, 256], P(('dp', 'mp')), may hold values from -0.15625 to 0.15625
- conv_x: bfloat16 [4, 3072], P(None, ('mp', 'dp')), may hold values from -3 to 3
- conv_x_bias: bfloat16 [3072], P(('mp', 'dp')), may hold values from -0.5 to 0.5
- conv_bc: bfloat16 [4, 256], P(None, ('dp', 'mp')), may hold values from -3 to 3
- conv_bc_bias: bfloat16 [256], P(('dp', 'mp')), may hold values from -0.5 to 0.5
- a_log: float32 [48], P('mp'), may hold values from 0 to 2.5
- d_skip: float32 [48], P('mp'), may hold values from 0.5 to 1.5
- dt_bias: float32 [48], P('mp'), may hold values from -7 to -2
- out_gain: bfloat16 [3072], P(('mp', 'dp')), may hold values from 0.5 to 1.5
- w_out: bfloat16 [3072, 1536], P('mp', 'dp'), may hold values from -0.109375 to 0.109375
Outputs:
- mixed: bfloat16 [32, 1024, 1536], P('dp', 'mp')
- grad_hidden: float32 [32, 1024, 1536], P('dp', 'mp')
- grad_norm_gain: float32 [1536], P(('dp', 'mp'))
- grad_w_z: float32 [1536, 3072], P('dp', 'mp')
- grad_w_x: float32 [1536, 3072], P('dp', 'mp')
- grad_w_dt: float32 [1536, 48], P('dp', 'mp')
- grad_w_bc: float32 [1536, 256], P(('dp', 'mp'))
- grad_conv_x: float32 [4, 3072], P(None, ('mp', 'dp'))
- grad_conv_x_bias: float32 [3072], P(('mp', 'dp'))
- grad_conv_bc: float32 [4, 256], P(None, ('dp', 'mp'))
- grad_conv_bc_bias: float32 [256], P(('dp', 'mp'))
- grad_a_log: float32 [48], P('mp')
- grad_d_skip: float32 [48], P('mp')
- grad_dt_bias: float32 [48], P('mp')
- grad_out_gain: float32 [3072], P(('mp', 'dp'))
- grad_w_out: float32 [3072, 1536], P('mp', 'dp')
The draws below stay inside these ranges and needn't reach their ends.
Inputs may be any that keep to these rules, and one draw needn't show every extreme that they name: `segments`: within each sequence the numbers start at 0 and rise by one at the first token of each document; every document has 200 to 1024 tokens.
All inputs are finite; a program needn't handle non-finite values.
Results may differ from the reference program's by a relative error of at most 0.012.
Values may be sent and summed in bfloat16 or wider, within the bound.
A program may use at most 192 MiB of HBM per device.

```python
import jax
import jax.numpy as jnp
from jax import lax

D = 1536
HEADS = 48
STATE = 128
CONV = 4
BLOCK = 256
SEQ_LEN = 1024
DOC_MIN = 200
SEQ_DP = 2
INNER = 3072
SEQS = 32


def draw_segments(key, part):
    key = jax.random.fold_in(key, 11)
    most_docs = SEQ_LEN // DOC_MIN
    key_pick, key_count, key_cut = jax.random.split(key, 3)
    chosen = jax.random.randint(key_pick, (SEQS // SEQ_DP,), 0, SEQ_DP)
    seq_index = jnp.arange(SEQS)
    single = seq_index % SEQ_DP == jnp.repeat(chosen, SEQ_DP)
    crowded = seq_index % SEQ_DP == jnp.repeat((chosen + 1) % SEQ_DP, SEQ_DP)
    doc_count = jnp.where(single, 1, jnp.where(crowded, most_docs, jax.random.randint(key_count, (SEQS,), 1, most_docs + 1)))
    spare_len = SEQ_LEN - doc_count * DOC_MIN
    cut_points = jax.random.randint(key_cut, (SEQS, max(most_docs - 1, 1)), 0, spare_len[:, None] + 1)
    cut_points = jnp.sort(cut_points, axis=1)
    doc_order = jnp.arange(1, max(most_docs - 1, 1) + 1)
    starts = jnp.where(doc_order[None, :] < doc_count[:, None], doc_order[None, :] * DOC_MIN + cut_points, SEQ_LEN)
    position = jnp.arange(SEQ_LEN)
    return jnp.sum((position[None, :, None] >= starts[:, None, :]).astype(jnp.int32), axis=2)


def block_levels(own_key, shape, cuts, smallest, top_value):
    level = 1.0
    for dim, shards_of in cuts:
        heights = jax.random.uniform(jax.random.fold_in(jax.random.fold_in(own_key, 6), dim), (shards_of,), jnp.float32, smallest / len(cuts), top_value / len(cuts))
        level = level * jnp.repeat(jnp.exp(heights), shape[dim] // shards_of).reshape((-1,) + (1,) * (len(shape) - 1 - dim))
    return level


def bell_draw(key, shape, deviation, bound, cuts=(), kind=jnp.bfloat16):
    drawn = deviation * jax.random.normal(key, shape, jnp.float32)
    if cuts:
        drawn = drawn * block_levels(key, shape, cuts, -0.22, 0.18)
    return jnp.clip(drawn, -bound, bound).astype(kind)


def setup_inputs(seed: int = 0) -> dict:
    splits = jax.random.split(jax.random.key(seed), 18)
    hidden = bell_draw(splits[0], (SEQS, SEQ_LEN, D), 1.0, 6.0, ((0, 16), (1, 8)))
    segments = draw_segments(jax.random.fold_in(splits[17], 71), 0)
    cotangent = bell_draw(splits[2], (SEQS, SEQ_LEN, D), 1.0, 6.0, ((0, 16), (1, 8)))
    norm_gain = jnp.clip(1.0 + 0.1 * jax.random.normal(splits[3], (D,), jnp.float32), 0.5, 1.5).astype(jnp.bfloat16)
    w_z = bell_draw(splits[4], (D, INNER), D ** -0.5, 0.15625, ((0, 16), (1, 8)))
    w_x = bell_draw(splits[5], (D, INNER), D ** -0.5, 0.15625, ((0, 16), (1, 8)))
    w_dt = bell_draw(splits[6], (D, HEADS), D ** -0.5, 0.15625, ((0, 16), (1, 8)))
    w_bc = bell_draw(splits[7], (D, 2 * STATE), D ** -0.5, 0.15625, ((0, 128),))
    conv_x = bell_draw(splits[8], (CONV, INNER), 0.5, 3.0, ((1, 128),))
    conv_x_bias = jnp.clip(jax.random.uniform(splits[9], (INNER,), jnp.float32, -0.5, 0.5) * block_levels(splits[9], (INNER,), ((0, 128),), -0.4, 0.0), -0.5, 0.5).astype(jnp.bfloat16)
    conv_bc = bell_draw(splits[10], (CONV, 2 * STATE), 0.5, 3.0, ((1, 128),))
    conv_bc_bias = jnp.clip(jax.random.uniform(splits[11], (2 * STATE,), jnp.float32, -0.5, 0.5) * block_levels(splits[11], (2 * STATE,), ((0, 128),), -0.4, 0.0), -0.5, 0.5).astype(jnp.bfloat16)
    a_log = jnp.clip(2.5 * jax.random.uniform(splits[12], (HEADS,), jnp.float32) ** block_levels(splits[12], (HEADS,), ((0, 8),), -0.2, 0.2), 0.0, 2.5)
    d_skip = jnp.clip(0.5 + 1.0 * jax.random.uniform(splits[13], (HEADS,), jnp.float32) ** block_levels(splits[13], (HEADS,), ((0, 8),), -0.2, 0.2), 0.5, 1.5)
    dt_bias = jnp.clip(-7.0 + 5.0 * jax.random.uniform(splits[14], (HEADS,), jnp.float32) ** block_levels(splits[14], (HEADS,), ((0, 8),), -0.2, 0.2), -7.0, -2.0)
    out_gain = jnp.clip(1.0 + 0.1 * jax.random.normal(splits[15], (INNER,), jnp.float32), 0.5, 1.5).astype(jnp.bfloat16)
    w_out = bell_draw(splits[16], (INNER, D), INNER ** -0.5, 0.109375, ((0, 8), (1, 16)))
    return {"hidden": hidden, "segments": segments, "cotangent": cotangent, "norm_gain": norm_gain, "w_z": w_z, "w_x": w_x, "w_dt": w_dt, "w_bc": w_bc, "conv_x": conv_x, "conv_x_bias": conv_x_bias, "conv_bc": conv_bc, "conv_bc_bias": conv_bc_bias, "a_log": a_log, "d_skip": d_skip, "dt_bias": dt_bias, "out_gain": out_gain, "w_out": w_out}


epsilon = 1e-05

@jax.custom_vjp
def low(v):
    return lax.optimization_barrier(v.astype(jnp.bfloat16)).astype(jnp.float32)

@jax.custom_vjp
def low_back(v):
    return v

def low_keep(v):
    return (low(v), None)

def low_pass(kept, grad):
    return (grad,)

def back_keep(v):
    return (v, None)

def back_low(kept, grad):
    return (low(grad),)
low.defvjp(low_keep, low_pass)
low_back.defvjp(back_keep, back_low)

def causal_conv(values, kernel, offset, seg_ids):
    length = values.shape[0]
    tap_count = kernel.shape[0]
    result = offset[None, :] + kernel[tap_count - 1][None, :] * values
    for shift_by in range(1, tap_count):
        moved = jnp.concatenate([jnp.zeros((shift_by, values.shape[1]), values.dtype), values[:length - shift_by]], 0)
        moved_ids = jnp.concatenate([jnp.full((shift_by,), -1, jnp.int32), seg_ids[:length - shift_by]], 0)
        keep_mask = jnp.where(moved_ids == seg_ids, 1.0, 0.0).astype(values.dtype)
        result = result + kernel[tap_count - 1 - shift_by][None, :] * moved * keep_mask[:, None]
    return result

def state_space(x_heads, step_size, log_decay, b_mat, c_mat, seg_ids):
    length, head_count, head_dim = x_heads.shape
    blocks = length // BLOCK
    highest = lax.Precision.HIGHEST

    def by_block(values):
        return values.reshape((blocks, BLOCK) + values.shape[1:])

    def one_block(carry, pieces):
        carried, last_id = carry
        x_blk, step_blk, decay_blk, b_blk, c_blk, id_blk = pieces
        cumulative = jnp.cumsum(decay_blk, axis=0)
        position = jnp.arange(BLOCK)
        same_doc = (id_blk[:, None] == id_blk[None, :]) & (position[:, None] >= position[None, :])
        decay_gaps = cumulative[:, None, :] - cumulative[None, :, :]
        decay_mat = jnp.exp(jnp.where(same_doc[:, :, None], decay_gaps, -10000.0))
        scores = jnp.dot(c_blk, b_blk.T, precision=highest)
        mix_weights = decay_mat * scores[:, :, None] * step_blk[None, :, :]
        inside = jnp.einsum('tsh,shp->thp', mix_weights, x_blk, precision=highest)
        enter_rate = jnp.exp(cumulative) * jnp.where(id_blk == last_id, 1.0, 0.0).astype(x_heads.dtype)[:, None]
        from_state = jnp.einsum('tn,hpn->thp', c_blk, carried, precision=highest) * enter_rate[:, :, None]
        tail_id = id_blk[BLOCK - 1]
        leave_rate = jnp.exp(jnp.where((id_blk == tail_id)[:, None], cumulative[BLOCK - 1][None, :] - cumulative, -10000.0)) * step_blk
        keep_rate = jnp.exp(cumulative[BLOCK - 1]) * jnp.where(tail_id == last_id, 1.0, 0.0).astype(x_heads.dtype)
        carried = carried * keep_rate[:, None, None] + jnp.einsum('sh,shp,sn->hpn', leave_rate, x_blk, b_blk, precision=highest)
        return ((carried, tail_id), inside + from_state)
    initial = (jnp.zeros((head_count, head_dim, b_mat.shape[1]), x_heads.dtype), jnp.array(-1, jnp.int32))
    ignored, outputs = lax.scan(jax.checkpoint(one_block), initial, (by_block(x_heads), by_block(step_size), by_block(log_decay), by_block(b_mat), by_block(c_mat), by_block(seg_ids)))
    return outputs.reshape(length, head_count, head_dim)

def ssd_mixer(z_in, x_in, dt_in, bc_in, kern_x, bias_x, kern_bc, bias_bc, log_rate, skip_gain, step_bias, seg_ids):
    length = z_in.shape[0]
    head_count = dt_in.shape[1]
    x_act = jax.nn.silu(causal_conv(x_in, kern_x, bias_x, seg_ids))
    bc_act = jax.nn.silu(causal_conv(bc_in, kern_bc, bias_bc, seg_ids))
    state_size = bc_act.shape[1] // 2
    step_size = jax.nn.softplus(dt_in + step_bias)
    log_decay = -jnp.exp(log_rate) * step_size
    x_heads = x_act.reshape(length, head_count, -1)
    y_heads = state_space(x_heads, step_size, log_decay, bc_act[:, :state_size], bc_act[:, state_size:], seg_ids) + skip_gain[None, :, None] * x_heads
    return y_heads.reshape(length, -1) * jax.nn.silu(z_in)

def block_layer(seq_rows, seg_ids, params):
    gain_in, proj_z, proj_x, proj_dt, proj_bc, kern_x, bias_x, kern_bc, bias_bc, log_rate, skip_gain, step_bias, gain_out, proj_out = params
    highest = lax.Precision.HIGHEST
    inv_rms = lax.rsqrt(lax.optimization_barrier(jnp.mean(seq_rows * seq_rows, -1, keepdims=True)) + epsilon)
    normed = low(seq_rows * inv_rms * gain_in)
    z_in = low_back(jnp.dot(normed, proj_z, precision=highest, preferred_element_type=jnp.float32))
    x_in = low_back(jnp.dot(normed, proj_x, precision=highest, preferred_element_type=jnp.float32))
    dt_in = low_back(jnp.dot(normed, proj_dt, precision=highest, preferred_element_type=jnp.float32))
    bc_in = low_back(jnp.dot(normed, proj_bc, precision=highest, preferred_element_type=jnp.float32))
    gated = ssd_mixer(z_in, x_in, dt_in, bc_in, kern_x, bias_x, kern_bc, bias_bc, log_rate, skip_gain, step_bias, seg_ids)
    out_scale = lax.rsqrt(lax.optimization_barrier(jnp.mean(gated * gated, -1, keepdims=True)) + epsilon)
    out_normed = low(gated * out_scale * gain_out)
    return seq_rows + jnp.dot(out_normed, proj_out, precision=highest, preferred_element_type=jnp.float32)

def reference(hidden, segments, cotangent, norm_gain, w_z, w_x, w_dt, w_bc, conv_x, conv_x_bias, conv_bc, conv_bc_bias, a_log, d_skip, dt_bias, out_gain, w_out):
    params = tuple((member.astype(jnp.float32) for member in (norm_gain, w_z, w_x, w_dt, w_bc, conv_x, conv_x_bias, conv_bc, conv_bc_bias, a_log, d_skip, dt_bias, out_gain, w_out)))

    def per_sequence(totals, inputs):
        seq_rows, seg_ids, cot_rows = inputs

        def forward(rows_in, weights):
            return block_layer(rows_in, seg_ids, weights)
        result, pullback = jax.vjp(forward, seq_rows.astype(jnp.float32), params)
        grad_rows, grad_params = pullback(cot_rows.astype(jnp.float32))
        totals = tuple((earlier + added for earlier, added in zip(totals, grad_params)))
        return (totals, (result.astype(jnp.bfloat16), grad_rows))
    zero_totals = tuple((jnp.zeros_like(member) for member in params))
    totals, outputs = lax.scan(per_sequence, zero_totals, (hidden, segments, cotangent))
    mixed, grad_hidden = outputs
    return (mixed, grad_hidden, totals[0], totals[1], totals[2], totals[3], totals[4], totals[5], totals[6], totals[7], totals[8], totals[9], totals[10], totals[11], totals[12], totals[13])
```

```python
import jax
import jax.numpy as jnp
from jax import lax
from jax.experimental import pallas as pl
from jax.experimental.pallas import tpu as pltpu
from jax.sharding import PartitionSpec as P

MESH = pl.DeviceIdType.MESH
EPS = 1e-05
Q = 128
HALO = 8
F32 = jnp.float32
BF16 = jnp.bfloat16
LOG2E = 1.4426950408889634
VMEM_LIMIT = 56 * 1024 * 1024

KEEP = 0
AHEAD = 4
SEG, ENTER, LEAVE, CARRY, SCALE, COEF = 8, 9, 10, 11, 12, 13
STEP_ROWS = 256

BC_TAPS, IN_GAIN, X_TAPS, HEAD_ROWS, SMALL_SHARED, SMALL_ROWS = 0, 10, 24, 60, 24, 64


def dot(a, b, dims=((1,), (0,))):
    return lax.dot_general(a, b, (dims, ((), ())), preferred_element_type=F32)


def dot_exact(a, b, dims=((1,), (0,))):
    return lax.dot_general(
        a, b, (dims, ((), ())), preferred_element_type=F32, precision=lax.Precision.HIGHEST
    )


NT = ((1,), (1,))
TN = ((0,), (0,))


def sigmoid(v):
    return 1.0 / (1.0 + jnp.exp(-v))


def softplus(v):
    return jnp.maximum(v, 0.0) + jnp.log1p(jnp.exp(-jnp.abs(v)))


def wide(small, row, count):
    return jnp.concatenate([small[row + i : row + i + 1] for i in range(count)], 1)


def columns_of(rows16):
    return jnp.concatenate([rows16, jnp.zeros((128 - rows16.shape[0], Q), F32)], 0).T


def lanes_of(tok, lane):
    return tok[:, lane : lane + 1]


def expand(values, width):
    rows = values.shape[0]
    first = lax.broadcasted_iota(jnp.int32, (rows, 128), 1) < 64
    pieces = []
    for pair in range(width // 128):
        a = jnp.broadcast_to(values[:, 2 * pair : 2 * pair + 1], (rows, 128))
        b = jnp.broadcast_to(values[:, 2 * pair + 1 : 2 * pair + 2], (rows, 128))
        pieces.append(jnp.where(first, a, b))
    return jnp.concatenate(pieces, 1)


def head_sums(values):
    width = values.shape[1]
    channel = lax.broadcasted_iota(jnp.int32, (width, 128), 0)
    lane = lax.broadcasted_iota(jnp.int32, (width, 128), 1)
    pick = jnp.where((channel >= lane * 64) & (channel < lane * 64 + 64), 1.0, 0.0).astype(BF16)
    high = values.astype(BF16)
    low = (values - high.astype(F32)).astype(BF16)
    return dot(high, pick) + dot(low, pick)


def rows8(values):
    total = values[0:8]
    for start in range(8, values.shape[0], 8):
        total = total + values[start : start + 8]
    return total


def causal():
    row = lax.broadcasted_iota(jnp.int32, (Q, Q), 0)
    col = lax.broadcasted_iota(jnp.int32, (Q, Q), 1)
    return row >= col


def pair_blocks(values):
    first = lax.broadcasted_iota(jnp.int32, values.shape, 1) < 64
    zero = jnp.zeros_like(values)
    return jnp.concatenate([jnp.where(first, values, zero), jnp.where(first, zero, values)], 0)


def decays(dt, hp, tok):
    step = softplus(dt + hp[2:3])
    rate = -jnp.exp(hp[0:1]) * step
    tri = jnp.where(causal(), 1.0, 0.0)
    cum = dot_exact(tri, rate)
    last = cum[Q - 1 : Q]
    enter = jnp.exp(cum) * lanes_of(tok, ENTER)
    leave = jnp.exp(last - cum) * lanes_of(tok, LEAVE)
    keep = jnp.exp(last) * tok[0:1, CARRY : CARRY + 1]
    cum2 = cum * LOG2E
    return step, rate, cum2, cum2.T, enter, leave, keep


def gaps(cum2, cum2_t, head):
    return jnp.exp2(jnp.minimum(cum2[:, head : head + 1] - cum2_t[head : head + 1, :], 0.0))


def place():
    dp, mp = lax.axis_index("dp"), lax.axis_index("mp")
    return {"xh": dp // 8, "z": (dp // 2) % 4, "c": dp % 2, "y": mp // 2, "xl": mp % 2}


def device(at, **other):
    at = {**at, **other}
    return (at["xh"] * 8 + at["z"] * 2 + at["c"], at["y"] * 2 + at["xl"])


def group_peers(at):
    peers = []
    for dy in range(4):
        for flip in range(2):
            if dy or flip:
                peers.append({**at, "y": (at["y"] + dy) % 4, "xl": (at["xl"] + flip) % 2})
    return peers


def x_peers(at):
    flips = [(0, 1), (1, 0), (1, 1)]
    return [{**at, "xh": (at["xh"] + a) % 2, "xl": (at["xl"] + b) % 2} for a, b in flips]


def z_peers(at):
    return [{**at, "z": (at["z"] + d) % 4} for d in range(1, 4)]


def y_peers(at):
    return [{**at, "y": (at["y"] + d) % 4} for d in range(1, 4)]


def core_peers(at):
    return [{**at, "c": 1 - at["c"]}]


def plane_peers(at):
    peers = z_peers(at)
    for x_peer in x_peers(at):
        peers += [x_peer] + z_peers(x_peer)
    return peers


def greet(peers):
    barrier = pltpu.get_barrier_semaphore()
    for peer in peers:
        pl.semaphore_signal(barrier, inc=1, device_id=device(peer), device_id_type=MESH)
    pl.semaphore_wait(barrier, len(peers))


class Sends:
    def __init__(self, send_sems, recv_sems):
        self.send_sems, self.recv_sems, self.used = send_sems, recv_sems, 0

    def make(self, source, target, peer):
        slot = self.used
        self.used += 1
        return pltpu.make_async_remote_copy(
            src_ref=source,
            dst_ref=target,
            send_sem=self.send_sems.at[slot],
            recv_sem=self.recv_sems.at[slot],
            device_id=device(peer),
            device_id_type=MESH,
        )

    def start(self, source, target, peer):
        copy = self.make(source, target, peer)
        copy.start()
        return copy


def start_all(copies):
    for copy in copies:
        copy.start()


def wait_all(copies):
    for copy in copies:
        copy.wait()


def here_copies(pairs, sems):
    copies = [pltpu.make_async_copy(a, b, sems.at[i]) for i, (a, b) in enumerate(pairs)]
    start_all(copies)
    return copies


def exchange(total, taken, peers, held, sends):
    copies = []
    for i, peer in enumerate(peers):
        copies.append(sends.start(total.at[0:taken], held.at[i, 0:taken], peer))
    wait_all(copies)
    add = total[0:taken]
    for i in range(len(peers)):
        add = add + held[i, 0:taken]
    total[0:taken] = add


class Layout:
    def __init__(self, width):
        self.width, self.half = width, width // 2
        self.part = self.half + 256
        self.total = 2 * self.part

    def x(self, v):
        return jnp.concatenate([v[:, : self.half], v[:, self.part : self.part + self.half]], 1)

    def bc(self, v):
        a, b = self.half, self.part + self.half
        return jnp.concatenate([v[:, a : a + 128], v[:, b : b + 128]], 1)

    def dt(self, v, own_heads):
        a, b = self.half + 128, self.part + self.half + 128
        return v[:, a : a + 128] + pltpu.roll(v[:, b : b + 128], own_heads, 1)

    def join(self, x, bc, dt, own_heads):
        lane = lax.broadcasted_iota(jnp.int32, dt.shape, 1)
        first = jnp.where(lane < own_heads, dt, 0.0)
        second = jnp.where(lane < own_heads, pltpu.roll(dt, 128 - own_heads, 1), 0.0)
        return jnp.concatenate(
            [x[:, : self.half], bc[:, :128], first, x[:, self.half :], bc[:, 128:], second], 1
        )


def own_heads_of(width):
    return width // 128


def chunk_rows(j):
    return pl.ds(pl.multiple_of(j * Q, Q), Q)


class RingGather:
    SEMS = 7

    def __init__(self, at, source, target, send_sems, recv_sems, local_sem):
        self.at, self.source, self.target = at, source, target
        self.sems = (send_sems, recv_sems)
        self.local_sem = local_sem
        self.up, self.down = {**at, "y": (at["y"] + 1) % 4}, {**at, "y": (at["y"] + 3) % 4}
        self.pair = {**at, "xl": 1 - at["xl"]}

    def rows(self, y, xl):
        return self.target.at[pl.ds(pl.multiple_of((y * 2 + xl) * Q, Q), Q)]

    def copies(self, stage):
        at = self.at
        y, xl, other = at["y"], at["xl"], 1 - at["xl"]
        sends = Sends(*self.sems)
        if stage == 0:
            mine = self.rows(y, xl)
            own = self.source.at[xl]
            return [sends.make(self.source.at[other], mine, self.pair)] + [
                sends.make(own, mine, p) for p in (self.up, self.down)
            ]
        if stage == 1:
            sends.used = 3
            got = self.rows(y, other)
            return [sends.make(got, got, p) for p in (self.up, self.down)]
        sends.used = 5
        low, high = self.rows((y + 3) % 4, xl), self.rows((y + 1) % 4, other)
        return [sends.make(low, low, self.up), sends.make(high, high, self.down)]

    def local(self):
        return pltpu.make_async_copy(self.source.at[self.at["xl"]], self.rows(self.at["y"], self.at["xl"]), self.local_sem)

    def begin(self):
        start_all(self.copies(0))
        self.local().start()

    def second(self):
        self.copies(0)[0].wait()
        start_all(self.copies(1))

    def third(self):
        wait_all(self.copies(0)[1:])
        wait_all(self.copies(1))
        start_all(self.copies(2))

    def finish(self):
        wait_all(self.copies(2))
        self.local().wait()


class RingScatter:
    SEMS = 7

    @staticmethod
    def scratch(width):
        return [pltpu.VMEM((12, Q, width), BF16), dma(RingScatter.SEMS), dma(RingScatter.SEMS), dma(4)]

    def __init__(self, at, part, refs):
        self.at, self.part = at, part
        self.held, self.ss, self.rs, self.ls = refs
        y = at["y"]
        self.up_y, self.down_y, self.far_y = (y + 1) % 4, (y + 3) % 4, (y + 2) % 4
        self.up, self.down = {**at, "y": self.up_y}, {**at, "y": self.down_y}
        self.pair = {**at, "xl": 1 - at["xl"]}

    def of(self, y, x):
        return self.part.at[y * 2 + x]

    def copies(self, stage):
        sends = Sends(self.ss, self.rs)
        held = self.held
        if stage == 0:
            return [
                sends.make(self.of(self.far_y, 0), held.at[0], self.up),
                sends.make(self.of(self.far_y, 1), held.at[1], self.down),
                sends.make(self.of(self.up_y, 1), held.at[2], self.up),
                sends.make(self.of(self.down_y, 0), held.at[3], self.down),
            ]
        if stage == 1:
            sends.used = 4
            return [sends.make(held.at[8], held.at[4], self.up), sends.make(held.at[9], held.at[5], self.down)]
        sends.used = 6
        return [sends.make(held.at[6], held.at[7], self.pair)]

    def locals(self):
        y = self.at["y"]
        sources = [self.of(self.up_y, 0), self.of(self.down_y, 1), self.of(y, 0), self.of(y, 1)]
        return [pltpu.make_async_copy(s, self.held.at[8 + i], self.ls.at[i]) for i, s in enumerate(sources)]

    def begin(self):
        start_all(self.copies(0))
        start_all(self.locals())

    def second(self):
        wait_all(self.locals())
        wait_all(self.copies(0)[:2])
        for i in range(2):
            self.held[8 + i] = (self.held[8 + i].astype(F32) + self.held[i].astype(F32)).astype(BF16)
        start_all(self.copies(1))

    def third(self, out):
        wait_all(self.copies(0)[2:])
        wait_all(self.copies(1))
        held, xl = self.held, self.at["xl"]
        totals = []
        for x in range(2):
            whole_part, summed = held[3 - x].astype(F32), held[4 + x].astype(F32)
            totals.append(held[10 + x].astype(F32) + whole_part + summed)
        out[xl] = jnp.where(xl == 0, totals[0], totals[1])
        held[6] = jnp.where(xl == 0, totals[1], totals[0]).astype(BF16)
        start_all(self.copies(2))

    def finish(self, out):
        wait_all(self.copies(2))
        out[1 - self.at["xl"]] = self.held[7].astype(F32)


def ring_greets(at):
    return [{**at, "y": (at["y"] + 1) % 4}, {**at, "y": (at["y"] + 3) % 4}, {**at, "xl": 1 - at["xl"]}]


class PlaneGather:
    SEMS = 13

    def __init__(self, at, source, target, send_sems, recv_sems, local_sem):
        self.at, self.source, self.target = at, source, target
        self.sems, self.local_sem = (send_sems, recv_sems), local_sem
        depth, half = source.shape[1], source.shape[2]
        self.upper, self.lower = pl.ds(0, depth // 2), pl.ds(depth // 2, depth // 2)
        self.cols = pl.ds(pl.multiple_of(at["xl"] * half, 128), half)

    def copies(self, stage):
        at, w = self.at, self.target
        xh, z, c = at["xh"], at["z"], at["c"]
        sends = Sends(*self.sems)
        if stage == 0:
            return [
                sends.make(self.source.at[:, self.upper], w.at[:, xh, z, c, self.upper, self.cols], p)
                for p in x_peers(at)
            ] + [
                sends.make(self.source.at[:, self.lower], w.at[:, xh, z, c, self.lower, self.cols], p)
                for p in z_peers(at)
            ]
        if stage == 1:
            sends.used = 6
            up, low = w.at[:, :, z, c, self.upper, :], w.at[:, xh, :, c, self.lower, self.cols]
            return [sends.make(up, up, p) for p in z_peers(at)] + [sends.make(low, low, p) for p in x_peers(at)]
        sends.used = 12
        slot = w.at[:, :, :, c]
        return [sends.make(slot, slot, core_peers(at)[0])]

    def local(self):
        at = self.at
        return pltpu.make_async_copy(
            self.source, self.target.at[:, at["xh"], at["z"], at["c"], :, self.cols], self.local_sem
        )

    def begin(self):
        start_all(self.copies(0))
        self.local().start()

    def second(self):
        self.local().wait()
        wait_all(self.copies(0))
        start_all(self.copies(1))

    def third(self):
        wait_all(self.copies(1))
        start_all(self.copies(2))

    def finish(self):
        wait_all(self.copies(2))


class Layout:
    def __init__(self, width):
        self.width, self.half = width, width // 2
        self.part = self.half + 256
        self.total = 2 * self.part

    def x(self, v):
        return jnp.concatenate([v[:, : self.half], v[:, self.part : self.part + self.half]], 1)

    def bc(self, v):
        a, b = self.half, self.part + self.half
        return jnp.concatenate([v[:, a : a + 128], v[:, b : b + 128]], 1)

    def dt(self, v, own_heads):
        a, b = self.half + 128, self.part + self.half + 128
        return v[:, a : a + 128] + pltpu.roll(v[:, b : b + 128], own_heads, 1)

    def join(self, x, bc, dt, own_heads):
        lane = lax.broadcasted_iota(jnp.int32, dt.shape, 1)
        first = jnp.where(lane < own_heads, dt, 0.0)
        second = jnp.where(lane < own_heads, pltpu.roll(dt, 128 - own_heads, 1), 0.0)
        return jnp.concatenate(
            [x[:, : self.half], bc[:, :128], first, x[:, self.half :], bc[:, 128:], second], 1
        )


def own_heads_of(width):
    return width // 128


def chunk_rows(j):
    return pl.ds(pl.multiple_of(j * Q, Q), Q)


def forward_kernel(
    tok_ref, small_ref, hid_ref, wxe_ref, cot_ref, w2_ref,
    z_ref, xe_ref, xc_ref, bcc_ref, y_ref, start_ref, gon_ref, normed_ref, cot_all_ref, w2_all_ref, stat_ref,
    state, xh, bch, cots, weights, normeds, ys, stats, held,
    cot_send, cot_recv, w_send, w_recv, stat_send, stat_recv, sems,
):
    step = pl.program_id(0)
    steps = pl.num_programs(0) // 2
    per_step = STEP_ROWS // Q
    width = z_ref.shape[1]
    lay = Layout(width)
    pairs = width // 128
    chunks = stats.shape[0] // 2
    own_heads = own_heads_of(width)
    at = place()
    ring = RingGather(at, cot_ref, cots, cot_send, cot_recv, sems.at[0])
    plane = PlaneGather(at, w2_ref, weights, w_send, w_recv, sems.at[1])

    def results():
        pairs_of = [(cots, cot_all_ref), (weights, w2_all_ref), (normeds, normed_ref)]
        return [pltpu.make_async_copy(a, b, sems.at[2 + i]) for i, (a, b) in enumerate(pairs_of)]

    @pl.when(step == 0)
    def _():
        greet(ring_greets(at) + y_peers(at)[1:2] + plane_greets(at))
        ring.begin()
        plane.begin()
        state[...] = jnp.zeros_like(state)
        xh[0:HALO] = jnp.zeros((HALO, width), F32)
        bch[0:HALO] = jnp.zeros((HALO, bch.shape[1]), F32)

    @pl.when(step == 1)
    def _():
        ring.second()
        plane.second()

    @pl.when(step == 2)
    def _():
        ring.third()

    @pl.when(step == 3)
    def _():
        plane.third()

    @pl.when(step == steps)
    def _():
        ring.finish()
        plane.finish()
        start_all(results())

    @pl.when(step < steps)
    def _():
        rows = hid_ref[...].astype(F32)
        inv_rms = lax.rsqrt(jnp.mean(rows * rows, -1, keepdims=True) + EPS)
        normed = (rows * inv_rms * wide(small_ref, IN_GAIN, 12)).astype(BF16)
        normeds[pl.ds(pl.multiple_of(step * STEP_ROWS, STEP_ROWS), STEP_ROWS)] = normed
        xe_ref[...] = dot(normed, wxe_ref[...])

        @pl.loop(0, per_step)
        def _(j):
            chunk = step * per_step + j
            here = chunk_rows(j)

            @pl.when(chunk > 0)
            def _():
                xh[0:HALO] = xh[Q : Q + HALO]
                bch[0:HALO] = bch[Q : Q + HALO]

            rows16 = tok_ref[chunk]
            tok = columns_of(rows16)
            hp = small_ref[HEAD_ROWS : HEAD_ROWS + 3]
            xe = xe_ref[here]

            def conv(held_rows, new, row, count):
                held_rows[HALO : HALO + Q] = new
                taps = [wide(small_ref, row + t * count, count) for t in range(5)]
                out = taps[4] + taps[3] * new
                for t in range(1, 4):
                    out = out + (taps[3 - t] * held_rows[HALO - t : HALO - t + Q]) * lanes_of(tok, KEEP + t)
                return out

            xc = conv(xh, lay.x(xe), X_TAPS, pairs)
            bcc = conv(bch, lay.bc(xe), BC_TAPS, 2)
            xc_ref[here] = xc
            bcc_ref[here] = bcc
            x_act = xc * sigmoid(xc)
            bc_act = bcc * sigmoid(bcc)
            n = bc_act.shape[1] // 2
            b_low = bc_act[:, :n].astype(BF16)
            c_low = bc_act[:, n:].astype(BF16)
            size, rate, cum2, cum2_t, enter, leave, keep = decays(lay.dt(xe, own_heads), hp, tok)
            same = causal() & (lanes_of(tok, SEG) == rows16[SEG : SEG + 1])
            scores = jnp.where(same, dot(c_low, b_low, NT), 0.0)
            xs = x_act * expand(size, width)
            xs_low = xs.astype(BF16)
            before = state[...]
            start_ref[j] = before
            inter = dot(c_low, before.astype(BF16)) * expand(enter, width)
            outs = []
            for pair in range(pairs):
                mixes = [(scores * gaps(cum2, cum2_t, 2 * pair + i)).astype(BF16) for i in range(2)]
                outs.append(
                    dot(jnp.concatenate(mixes, 1), pair_blocks(xs_low[:, pair * 128 : pair * 128 + 128]))
                )
            skip = expand(jnp.broadcast_to(hp[1:2], (8, 128)), width)[0:1]
            y = jnp.concatenate(outs, 1) + inter + skip * x_act
            y_ref[here] = y
            ys[chunk_rows(chunk)] = y
            moved = (xs * expand(leave, width)).astype(BF16)
            keep_all = expand(jnp.broadcast_to(keep, (8, 128)), width)[0:1]
            state[...] = before * keep_all + dot(b_low, moved, TN)

    @pl.when(step >= steps)
    def _():
        rows = pl.ds(pl.multiple_of((step - steps) * STEP_ROWS, STEP_ROWS), STEP_ROWS)
        full = weights.shape[1] * weights.shape[2] * weights.shape[3] * weights.shape[4]
        z = dot(normeds[rows], weights[0].reshape(full, width))
        gon = dot(cots[rows], weights[1].reshape(full, width))
        z_ref[...] = z
        gon_ref[...] = gon
        gated = ys[rows] * (z * sigmoid(z))
        inner = gated * (gon * wide(small_ref, X_TAPS + 5 * pairs, pairs))
        for j in range(per_step):
            chunk = (step - steps) * per_step + j
            cut = slice(j * Q, j * Q + Q)
            stats[pl.ds(chunk, 1), :] = row_sums(gated[cut] * gated[cut])
            stats[pl.ds(chunks + chunk, 1), :] = row_sums(inner[cut])

    @pl.when(step == 2 * steps - 1)
    def _():
        wait_all(results())
        exchange(stats, stats.shape[0], y_peers(at), held, Sends(stat_send, stat_recv))
        inner = width * 4
        scale = lax.rsqrt(stats[0:chunks] / inner + EPS)
        stat_ref[0:chunks] = scale
        stat_ref[chunks : 2 * chunks] = scale * scale * scale * stats[chunks : 2 * chunks] / inner


def row_sums(values):
    total = values[:, 0:128]
    for start in range(128, values.shape[1], 128):
        total = total + values[:, start : start + 128]
    return jnp.sum(total.T, axis=0, keepdims=True)


def half_of(value, xl):
    half = value.shape[-1] // 2
    return jnp.where(xl == 0, value[..., :half], value[..., half:])


class PlaneSum:
    SEMS = 13

    @staticmethod
    def scratch(count, depth, width):
        cut, half = depth // 2, width // 2
        return [
            pltpu.VMEM((count, 2, 4, depth, width), BF16),
            pltpu.VMEM((count, 2, 4, depth, width), BF16),
            pltpu.VMEM((3, count, 4, cut, half), BF16),
            pltpu.VMEM((3, count, 2, cut, width), BF16),
            pltpu.VMEM((count, 4, cut, half), BF16),
            pltpu.VMEM((count, 2, cut, width), BF16),
            pltpu.VMEM((3, count, cut, half), BF16),
            pltpu.VMEM((3, count, cut, half), BF16),
            pltpu.SemaphoreType.DMA((PlaneSum.SEMS,)),
            pltpu.SemaphoreType.DMA((PlaneSum.SEMS,)),
            pltpu.SemaphoreType.DMA((1,)),
        ]

    def __init__(self, at, source, refs):
        self.at, self.source = at, source
        (self.mine, self.got, self.a2, self.b2, self.sa, self.sb, self.a3, self.b3, self.ss, self.rs, self.ls) = refs
        self.count, self.depth, self.width = self.mine.shape[0], self.mine.shape[3], self.mine.shape[4]
        self.cut, self.half = self.depth // 2, self.width // 2

    def columns(self, xl):
        return pl.ds(pl.multiple_of(xl * self.half, 128), self.half)

    def sends(self, used):
        sends = Sends(self.ss, self.rs)
        sends.used = used
        return sends

    def local(self):
        return pltpu.make_async_copy(self.source.at[:, :, :, self.at["c"]], self.mine, self.ls.at[0])

    def first(self):
        peer = core_peers(self.at)[0]
        return [self.sends(0).make(self.source.at[:, :, :, peer["c"]], self.got, peer)]

    def second(self):
        sends = self.sends(1)
        upper, lower = pl.ds(0, self.cut), pl.ds(self.cut, self.cut)
        copies = []
        for i, p in enumerate(x_peers(self.at)):
            copies.append(
                sends.make(self.mine.at[:, p["xh"], :, upper, self.columns(p["xl"])], self.a2.at[i], p)
            )
        for i, p in enumerate(z_peers(self.at)):
            copies.append(sends.make(self.mine.at[:, :, p["z"], lower, :], self.b2.at[i], p))
        return copies

    def third(self):
        sends = self.sends(7)
        copies = []
        for i, p in enumerate(z_peers(self.at)):
            copies.append(sends.make(self.sa.at[:, p["z"]], self.a3.at[i], p))
        for i, p in enumerate(x_peers(self.at)):
            copies.append(sends.make(self.sb.at[:, p["xh"], :, self.columns(p["xl"])], self.b3.at[i], p))
        return copies

    def begin(self):
        self.local().start()
        start_all(self.first())

    def after_cores(self):
        self.local().wait()
        wait_all(self.first())
        for m in range(self.count):
            for xh in range(2):

                @pl.loop(0, 4)
                def _(z):
                    total = self.mine[m, xh, z].astype(F32) + self.got[m, xh, z].astype(F32)
                    self.mine[m, xh, z] = total.astype(BF16)

        start_all(self.second())

    def after_first_axis(self):
        wait_all(self.second())
        at, cut = self.at, self.cut
        for m in range(self.count):

            @pl.loop(0, 4)
            def _(z):
                total = half_of(self.mine[m, at["xh"], z, 0:cut], at["xl"]).astype(F32)
                for i in range(3):
                    total = total + self.a2[i, m, z].astype(F32)
                self.sa[m, z] = total.astype(BF16)

            for xh in range(2):
                total = self.mine[m, xh, at["z"], cut : 2 * cut].astype(F32)
                for i in range(3):
                    total = total + self.b2[i, m, xh].astype(F32)
                self.sb[m, xh] = total.astype(BF16)
        start_all(self.third())

    def finish(self, out):
        wait_all(self.third())
        at, cut = self.at, self.cut
        for m in range(self.count):
            total = self.sa[m, at["z"]].astype(F32)
            for i in range(3):
                total = total + self.a3[i, m].astype(F32)
            out[m, 0:cut] = total
            total = half_of(self.sb[m, at["xh"]], at["xl"]).astype(F32)
            for i in range(3):
                total = total + self.b3[i, m].astype(F32)
            out[m, cut : 2 * cut] = total


def plane_greets(at):
    return x_peers(at)[1:] + z_peers(at) + core_peers(at)


def backward_kernel(
    tok_ref, stat_ref, small_ref, z_ref, xe_ref, gon_ref, xc_ref, bcc_ref, y_ref, start_ref, part_ref, g_ref,
    xel_ref, gkx_ref, gkbc_ref, ghead_ref, out_ref, gsum_ref,
    adjoint, dh, dbh, *refs,
):
    turn = pl.program_id(0)
    turns = pl.num_programs(0)
    per_step = STEP_ROWS // Q
    width = z_ref.shape[1]
    lay = Layout(width)
    pairs = width // 128
    own_heads = own_heads_of(width)
    chunks = tok_ref.shape[0]
    at = place()
    ring = RingScatter(at, part_ref, refs[:4])
    plane = PlaneSum(at, g_ref, refs[4:])

    @pl.when(turn == 0)
    def _():
        greet(ring_greets(at) + plane_greets(at))
        ring.begin()
        plane.begin()
        adjoint[...] = jnp.zeros_like(adjoint)
        dh[...] = jnp.zeros_like(dh)
        dbh[...] = jnp.zeros_like(dbh)
        gkx_ref[...] = jnp.zeros_like(gkx_ref)
        gkbc_ref[...] = jnp.zeros_like(gkbc_ref)
        ghead_ref[...] = jnp.zeros_like(ghead_ref)

    @pl.when(turn == 1)
    def _():
        plane.after_cores()

    @pl.when(turn == 2)
    def _():
        ring.second()

    @pl.when(turn == turns - 1)
    def _():
        plane.after_first_axis()

    @pl.loop(0, per_step)
    def _(turn_in):
        j = per_step - 1 - turn_in
        chunk = (turns - 1 - turn) * per_step + j
        here = chunk_rows(j)

        @pl.when(chunk < chunks - 1)
        def _():
            dh[Q : Q + HALO] = dh[0:HALO]
            dbh[Q : Q + HALO] = dbh[0:HALO]

        rows16 = tok_ref[chunk]
        rows16 = jnp.concatenate(
            [rows16[0:SCALE], stat_ref[pl.ds(chunk, 1), :], stat_ref[pl.ds(chunks + chunk, 1), :], rows16[14:16]], 0
        )
        tok = columns_of(rows16)
        hp = small_ref[HEAD_ROWS : HEAD_ROWS + 3]
        xe = xe_ref[here]
        dt_in = lay.dt(xe, own_heads)
        xc = xc_ref[here]
        bcc = bcc_ref[here]
        x_sig = sigmoid(xc)
        x_act = xc * x_sig
        bc_sig = sigmoid(bcc)
        bc_act = bcc * bc_sig
        n = bc_act.shape[1] // 2
        b_low = bc_act[:, :n].astype(BF16)
        c_low = bc_act[:, n:].astype(BF16)
        size, rate, cum2, cum2_t, enter, leave, keep = decays(dt_in, hp, tok)
        same = causal() & (lanes_of(tok, SEG) == rows16[SEG : SEG + 1])
        scores = jnp.where(same, dot(c_low, b_low, NT), 0.0)
        step_all = expand(size, width)
        leave_all = expand(leave, width)
        xs = x_act * step_all
        xs_low = xs.astype(BF16)
        moved = (xs * leave_all).astype(BF16)

        z = z_ref[here]
        z_act = z * sigmoid(z)
        y = y_ref[here]
        gated = y * z_act
        gon = gon_ref[here]
        scale = lanes_of(tok, SCALE)
        gain = wide(small_ref, X_TAPS + 5 * pairs, pairs)
        grad_gated = scale * (gon * gain) - gated * lanes_of(tok, COEF)
        gkx_ref[5] += rows8(gon * gated * scale)
        dy = grad_gated * z_act
        dy_low = dy.astype(BF16)
        dy_in = (dy * expand(enter, width)).astype(BF16)

        skip = expand(jnp.broadcast_to(hp[1:2], (8, 128)), width)[0:1]
        before = start_ref[j]
        before_low = before.astype(BF16)
        after = adjoint[...]
        after_low = after.astype(BF16)

        from_state = dot(b_low, after_low)
        outs = []
        dscores = jnp.zeros((Q, Q), F32)
        for pair in range(pairs):
            cut = slice(pair * 128, pair * 128 + 128)
            dys = pair_blocks(dy_low[:, cut])
            inner = dot(dys, xs_low[:, cut], NT)
            mixes = []
            for i in range(2):
                gap = gaps(cum2, cum2_t, 2 * pair + i)
                mixes.append((scores * gap).astype(BF16))
                dscores = dscores + inner[i * Q : i * Q + Q] * gap
            outs.append(dot(jnp.concatenate(mixes, 0), dys, TN))
        intra = jnp.concatenate(outs, 1)
        dscores = jnp.where(same, dscores, 0.0).astype(BF16)

        dxs = intra + leave_all * from_state
        dx_act = dxs * step_all + skip * dy
        gkx_ref[6] += rows8(dy * x_act)
        plus = head_sums(dy_low.astype(F32) * (y - skip * x_act))
        through = moved.astype(F32) * from_state
        minus = head_sums(xs_low.astype(F32) * intra + through)
        direct = head_sums(dxs * x_act)
        keep_all = expand(jnp.broadcast_to(keep, (8, 128)), width)[0:1]
        at_end = rows8(through) + keep_all * rows8(after * before)
        at_end = jnp.sum(head_sums(at_end), axis=0, keepdims=True)
        last_row = lax.broadcasted_iota(jnp.int32, (Q, 128), 0) == Q - 1
        dcum = plus - minus + jnp.where(last_row, at_end, 0.0)
        tri = jnp.where(causal(), 1.0, 0.0)
        drate = dot_exact(tri, dcum, TN)
        dstep = direct - jnp.exp(hp[0:1]) * drate
        ddt = dstep * sigmoid(dt_in + hp[2:3])
        ghead_ref[0] += rows8(drate * rate)
        ghead_ref[1] += rows8(ddt)

        dc = dot(dscores, b_low) + dot(dy_in, before_low, NT)
        db = dot(dscores, c_low, TN) + dot(moved, after_low, NT)
        adjoint[...] = keep_all * after + dot(c_low, dy_in, TN)

        def conv_back(held, grad, new, row, count, out_ref):
            held[0:Q] = grad
            taps = [wide(small_ref, row + t * count, count) for t in range(4)]
            total = taps[3] * grad
            out_ref[3] += rows8(new * grad)
            out_ref[4] += rows8(grad)
            for t in range(1, 4):
                part = held[t : t + Q] * lanes_of(tok, AHEAD + t)
                total = total + taps[3 - t] * part
                out_ref[3 - t] += rows8(new * part)
            return total

        dxc = dx_act * (x_sig * (1.0 + xc * (1.0 - x_sig)))
        dx_in = conv_back(dh, dxc, lay.x(xe), X_TAPS, pairs, gkx_ref)
        dbcc = jnp.concatenate([db, dc], 1) * (bc_sig * (1.0 + bcc * (1.0 - bc_sig)))
        dbc_in = conv_back(dbh, dbcc, lay.bc(xe), BC_TAPS, 2, gkbc_ref)
        xel_ref[here] = lay.join(dx_in, dbc_in, ddt, own_heads).astype(BF16)

    @pl.when(turn == turns - 1)
    def _():
        ring.third(out_ref)
        plane.finish(gsum_ref)
        ring.finish(out_ref)


def put_wide(ref, row, value):
    for i in range(value.shape[1] // 128):
        ref[row + i : row + i + 1] = value[:, i * 128 : i * 128 + 128]


def end_kernel(
    part_ref, g_ref, gain_ref, gkx_ref, gkbc_ref, ghead_ref,
    out_ref, gsum_ref, sums_ref, bcs_ref,
    held, small_send, small_recv, bc_send, bc_recv, *refs,
):
    at = place()
    ring = RingScatter(at, part_ref, refs[:4])
    plane = PlaneSum(at, g_ref, refs[4:])
    peers = group_peers(at)
    greet(peers + plane_greets(at))
    ring.begin()
    plane.begin()
    sums_ref[...] = jnp.zeros_like(sums_ref)
    for t in range(5):
        put_wide(sums_ref, 2 * t, jnp.sum(gkbc_ref[t], axis=0, keepdims=True))
    put_wide(sums_ref, IN_GAIN, gain_ref[...])
    pairs = gkx_ref.shape[2] // 128
    for t in range(7):
        put_wide(sums_ref, X_TAPS + t * pairs, jnp.sum(gkx_ref[t], axis=0, keepdims=True))
    for t in range(2):
        put_wide(sums_ref, X_TAPS + 7 * pairs + t, jnp.sum(ghead_ref[t], axis=0, keepdims=True))
    steps = [core_peers(at), x_peers(at), z_peers(at), y_peers(at)]
    sends = Sends(small_send, small_recv)
    rows = sums_ref.shape[0]
    exchange(sums_ref, rows, steps[0], held.at[0], sends)
    plane.after_cores()
    ring.second()
    exchange(sums_ref, rows, steps[1], held.at[1], sends)
    exchange(sums_ref, rows, steps[2], held.at[2], sends)
    plane.after_first_axis()
    exchange(sums_ref, SMALL_SHARED, steps[3], held.at[3], sends)
    ring.third(out_ref)
    plane.finish(gsum_ref)
    half = gsum_ref.shape[2] - 256
    bcs_ref[at["xl"], at["y"]] = gsum_ref[0, :, half : half + 128]
    slot = bcs_ref.at[at["xl"], at["y"]]
    sends = Sends(bc_send, bc_recv)
    wait_all([sends.start(slot, slot, p) for p in peers])
    ring.finish(out_ref)


def gather_kernel(
    hid, wx_ref, wdt_ref, wbc_ref, gain_ref, kx_ref, kxb_ref, kbc_ref, kbcb_ref, og_ref, al_ref, ds_ref, db_ref,
    hid_all, wxe_all, small_all,
    wxe, bc_got, bc_rows, held, lanes,
    hid_send, hid_recv, bc_send, bc_recv, w_send, w_recv, small_send, small_recv, sems,
):
    at = place()
    peers = group_peers(at)
    core, ys = core_peers(at), y_peers(at)
    greet(peers + plane_greets(at))
    ring = RingGather(at, hid, hid_all, hid_send, hid_recv, sems.at[0])
    plane = PlaneGather(at, wxe, wxe_all, w_send, w_recv, sems.at[1])
    ring.begin()
    y, xl = at["y"], at["xl"]
    bc_got[y * 2 + xl, 0:12] = wbc_ref[...].astype(F32)
    bc_slot = bc_got.at[y * 2 + xl]
    sends = Sends(bc_send, bc_recv)
    bc_copies = [sends.start(bc_slot, bc_slot, p) for p in peers]

    depth, half = wx_ref.shape
    own_heads = wdt_ref.shape[1]
    wxe[0, :, 0:half] = wx_ref[...]
    wxe[0, :, half + 128 : half + 256] = jnp.zeros((depth, 128), BF16)
    wxe[0, :, half + 128 : half + 128 + own_heads] = wdt_ref[...]

    def placed(pieces, width, start):
        lanes[...] = jnp.zeros_like(lanes)
        row = 0
        for piece in pieces:
            count, size = piece.shape
            lanes[row : row + count, 0:size] = piece[...].astype(F32)
            row += count
        return pltpu.roll(lanes[:, 0:width], start, 1)

    dp = at["xh"] * 8 + at["z"] * 2 + at["c"]
    everyone = dp * 8 + y * 2 + xl
    small_all[...] = jnp.zeros_like(small_all)
    value = placed([kbc_ref, kbcb_ref], 256, everyone * kbc_ref.shape[1])
    for t in range(5):
        put_wide(small_all, BC_TAPS + 2 * t, value[t : t + 1])
    value = placed([gain_ref], lanes.shape[1], everyone * gain_ref.shape[1])
    put_wide(small_all, IN_GAIN, value[0:1])
    value = placed([kx_ref, kxb_ref, og_ref], 2 * half, xl * half + dp * kx_ref.shape[1])
    for t in range(6):
        put_wide(small_all, X_TAPS + t * (half // 64), value[t : t + 1])
    value = placed([al_ref, ds_ref, db_ref], 128, xl * own_heads)
    small_all[HEAD_ROWS : HEAD_ROWS + 3] = jnp.where(dp == 0, value[0:3], 0.0)
    small_sends = Sends(small_send, small_recv)
    exchange(small_all, SMALL_SHARED, ys, held.at[0], small_sends)

    wait_all(bc_copies)
    for m in range(8):
        bc_rows[12 * m : 12 * m + 12] = bc_got[m, 0:12]
    wxe[0, :, half : half + 128] = half_of(bc_rows[...], xl).astype(BF16)
    plane.begin()
    exchange(small_all, SMALL_ROWS, core, held.at[1], small_sends)
    ring.second()
    plane.second()
    exchange(small_all, SMALL_ROWS, x_peers(at), held.at[2], small_sends)
    ring.third()
    exchange(small_all, SMALL_ROWS, z_peers(at), held.at[3], small_sends)
    plane.third()
    plane.finish()
    ring.finish()


def block(rows, w, index):
    return pl.BlockSpec((rows, w), lambda i: (index(i), 0))


def whole(shape):
    return pl.BlockSpec(shape, lambda i: (0,) * len(shape), pipeline_mode=pl.Buffered(1))


def whole_out(shape):
    return pl.BlockSpec(shape, lambda i: (0,) * len(shape))


ANY = pl.BlockSpec(memory_space=pl.ANY)
IN_VMEM = pl.BlockSpec(memory_space=pltpu.VMEM)


def like(shape, dtype):
    return jax.ShapeDtypeStruct(shape, dtype)


def dma(count):
    return pltpu.SemaphoreType.DMA((count,))


def remote_params(cid):
    return pltpu.CompilerParams(collective_id=cid, has_side_effects=True, vmem_limit_bytes=VMEM_LIMIT)


def gather_call(hidden, w_x, w_dt, w_bc, small_args):
    _, rows, model = hidden.shape
    depth, half = w_x.shape
    part = half + 256
    args = [w_x, w_dt, w_bc, *small_args]
    return pl.pallas_call(
        gather_kernel,
        in_specs=[ANY] + [IN_VMEM] * len(args),
        out_specs=[ANY, ANY, IN_VMEM],
        out_shape=[
            like((8 * rows, model), BF16),
            like((1, 2, 4, 2, depth, 2 * part), BF16),
            like((SMALL_ROWS, 128), F32),
        ],
        scratch_shapes=[
            pltpu.VMEM((1, depth, part), BF16),
            pltpu.VMEM((8, 16, w_bc.shape[1]), F32),
            pltpu.VMEM((depth, w_bc.shape[1]), F32),
            pltpu.VMEM((4, 3, SMALL_ROWS, 128), F32),
            pltpu.VMEM((8, model), F32),
            dma(7), dma(7), dma(7), dma(7), dma(13), dma(13), dma(10), dma(10), dma(2),
        ],
        name="gather",
        compiler_params=remote_params(0),
    )(hidden, *args)


def forward_call(tok, small, hid_all, wxe, cotangent, w2):
    length, model = hid_all.shape
    total = wxe.shape[1]
    depth, half = w2.shape[1], w2.shape[2]
    width = 2 * half
    steps = length // STEP_ROWS
    chunks = length // Q

    def early(i):
        return jnp.minimum(i, steps - 1)

    def late(i):
        return jnp.maximum(i - steps, 0)

    return pl.pallas_call(
        forward_kernel,
        grid=(2 * steps,),
        in_specs=[whole(tok.shape), whole(small.shape), block(STEP_ROWS, model, early), whole(wxe.shape), ANY, ANY],
        out_specs=[block(STEP_ROWS, width, late), block(STEP_ROWS, total, early), block(STEP_ROWS, width, early),
                   block(STEP_ROWS, 256, early), block(STEP_ROWS, width, early),
                   pl.BlockSpec((STEP_ROWS // Q, 128, width), lambda i: (early(i), 0, 0)),
                   block(STEP_ROWS, width, late), ANY, ANY, ANY, whole_out((2 * chunks, Q))],
        out_shape=[
            like((length, width), F32), like((length, total), F32), like((length, width), F32),
            like((length, 256), F32), like((length, width), F32), like((chunks, 128, width), F32),
            like((length, width), F32), like((length, model), BF16), like((length, model), BF16),
            like((2, 2, 4, 2, depth, width), BF16), like((2 * chunks, Q), F32),
        ],
        scratch_shapes=[
            pltpu.VMEM((128, width), F32),
            pltpu.VMEM((Q + HALO, width), F32),
            pltpu.VMEM((Q + HALO, 256), F32),
            pltpu.VMEM((length, model), BF16),
            pltpu.VMEM((2, 2, 4, 2, depth, width), BF16),
            pltpu.VMEM((length, model), BF16),
            pltpu.VMEM((length, width), F32),
            pltpu.VMEM((2 * chunks, Q), F32),
            pltpu.VMEM((3, 2 * chunks, Q), F32),
            dma(7), dma(7), dma(13), dma(13), dma(3), dma(3), dma(5),
        ],
        name="mix_forward",
        compiler_params=remote_params(1),
    )(tok, small, hid_all, wxe, cotangent, w2)


def backward_call(tok, stat, small, z, xe, gon, xc, bcc, y, starts, part_out, g):
    length, width = z.shape
    total = xe.shape[1]
    steps = length // STEP_ROWS
    count, depth = g.shape[0], g.shape[4]

    def back(i):
        return steps - 1 - i

    return pl.pallas_call(
        backward_kernel,
        grid=(steps,),
        in_specs=[whole(tok.shape), whole(stat.shape), whole(small.shape),
                  block(STEP_ROWS, width, back), block(STEP_ROWS, total, back), block(STEP_ROWS, width, back),
                  block(STEP_ROWS, width, back), block(STEP_ROWS, 256, back), block(STEP_ROWS, width, back),
                  pl.BlockSpec((STEP_ROWS // Q, 128, width), lambda i: (back(i), 0, 0)), ANY, ANY],
        out_specs=[block(STEP_ROWS, total, back), whole_out((7, 8, width)), whole_out((5, 8, 256)),
                   whole_out((2, 8, 128)), whole_out((2,) + part_out.shape[1:]),
                   whole_out((count, depth, width // 2))],
        out_shape=[
            like((length, total), BF16), like((7, 8, width), F32), like((5, 8, 256), F32), like((2, 8, 128), F32),
            like((2,) + part_out.shape[1:], F32), like((count, depth, width // 2), F32),
        ],
        scratch_shapes=[
            pltpu.VMEM((128, width), F32),
            pltpu.VMEM((Q + HALO, width), F32),
            pltpu.VMEM((Q + HALO, 256), F32),
            *RingScatter.scratch(part_out.shape[2]),
            *PlaneSum.scratch(count, depth, width),
        ],
        name="mix_backward",
        compiler_params=remote_params(2),
    )(tok, stat, small, z, xe, gon, xc, bcc, y, starts, part_out, g)


def end_call(part_in, g, gain, gkx, gkbc, ghead):
    count, depth, total = g.shape[0], g.shape[4], g.shape[5]
    return pl.pallas_call(
        end_kernel,
        in_specs=[ANY, ANY, IN_VMEM, IN_VMEM, IN_VMEM, IN_VMEM],
        out_specs=[IN_VMEM] * 4,
        out_shape=[
            like((2,) + part_in.shape[1:], F32),
            like((count, depth, total // 2), F32),
            like((72, 128), F32),
            like((2, 4, depth, 128), F32),
        ],
        scratch_shapes=[
            pltpu.VMEM((4, 3, 72, 128), F32),
            dma(10), dma(10), dma(7), dma(7),
            *RingScatter.scratch(part_in.shape[2]),
            *PlaneSum.scratch(count, depth, total),
        ],
        name="end",
        compiler_params=remote_params(3),
    )(part_in, g, gain, gkx, gkbc, ghead)


def token_info(ids):
    length = ids.shape[0]
    chunks = length // Q
    seg = ids.astype(F32)
    rows = [jnp.zeros((chunks, Q), F32)] * 16
    for j in range(1, 4):
        back = jnp.concatenate([jnp.full((j,), -1.0, F32), seg[:-j]])
        ahead = jnp.concatenate([seg[j:], jnp.full((j,), -1.0, F32)])
        rows[KEEP + j] = (back == seg).astype(F32).reshape(chunks, Q)
        rows[AHEAD + j] = (ahead == seg).astype(F32).reshape(chunks, Q)
    by_chunk = seg.reshape(chunks, Q)
    tail = by_chunk[:, Q - 1 :]
    last = jnp.concatenate([jnp.full((1, 1), -1.0, F32), tail[:-1]], 0)
    rows[SEG] = by_chunk
    rows[ENTER] = (by_chunk == last).astype(F32)
    rows[LEAVE] = (by_chunk == tail).astype(F32)
    rows[CARRY] = jnp.broadcast_to((tail == last).astype(F32), by_chunk.shape)
    return jnp.stack(rows, 1)


def local(
    hidden, segments, cotangent, norm_gain, w_z, w_x, w_dt, w_bc, conv_x, conv_x_bias, conv_bc, conv_bc_bias,
    a_log, d_skip, dt_bias, out_gain, w_out,
):
    at = place()
    y, xl = at["y"], at["xl"]
    dp, mp = lax.axis_index("dp"), lax.axis_index("mp")
    _, own_len, model = hidden.shape
    depth, half = w_z.shape
    width = 2 * half
    own_heads = a_log.shape[0]
    heads = 2 * own_heads
    lay = Layout(width)

    everyone = dp * 8 + mp
    small_args = [
        norm_gain[None], conv_x, conv_x_bias[None], conv_bc, conv_bc_bias[None], out_gain[None],
        a_log[None], d_skip[None], dt_bias[None],
    ]
    hid_all, wxe_all, small = gather_call(hidden, w_x, w_dt, w_bc, small_args)
    full_xe = wxe_all.reshape(model, lay.total)
    w2 = jnp.stack([w_z, w_out.T])

    ids = lax.dynamic_index_in_dim(segments, xl, 0, keepdims=False)
    tok = token_info(ids)
    z_in, xe_in, xc, bcc, y_out, starts, gon, normed, cot_all, w2_all, stat = forward_call(
        tok, small, hid_all, full_xe, cotangent, w2
    )
    w2_all = w2_all.reshape(2, model, width)
    full_z, full_o = w2_all[0], w2_all[1]

    gain_out = small[X_TAPS + 5 * (width // 128) : X_TAPS + 6 * (width // 128)].reshape(width)
    scale, coef = stat.reshape(2, -1, 1)[0], stat.reshape(2, -1, 1)[1]
    z_sig = sigmoid(z_in)
    z_act = z_in * z_sig
    gated = y_out * z_act
    out_normed = (gated * scale * gain_out).astype(BF16)
    grad_gated = scale * (gon * gain_out) - gated * coef
    z_low = (grad_gated * y_out * (z_sig * (1.0 + z_in * (1.0 - z_sig)))).astype(BF16)
    part_out = dot(out_normed, full_o, NT).astype(BF16).reshape(8, own_len, model)
    g_z = dot(normed, z_low, TN).astype(BF16)
    g_o = dot(cot_all, out_normed, TN).astype(BF16)
    g_zo = jnp.stack([g_z, g_o]).reshape(2, 2, 4, 2, depth, width)
    xe_low, gkx, gkbc, ghead, got_out, zo_sum = backward_call(
        tok, stat, small, z_in, xe_in, gon, xc, bcc, y_out, starts, part_out, g_zo
    )
    mixed = (hidden.astype(F32) + got_out).astype(BF16)

    part_in = dot(z_low, full_z, NT) + dot(xe_low, full_xe, NT)
    rows = hid_all.astype(F32)
    inv_rms = lax.rsqrt(jnp.mean(rows * rows, -1, keepdims=True) + EPS)
    g_gain = jnp.sum(part_in * (rows * inv_rms), 0)
    g_xe = dot(normed, xe_low, TN).astype(BF16).reshape(1, 2, 4, 2, depth, lay.total)
    grad_normed, xe_sum, sums, bc_sum = end_call(
        part_in.astype(BF16).reshape(8, own_len, model), g_xe, g_gain[None], gkx, gkbc, ghead
    )
    xe_sum = xe_sum[0]
    bc_sum = jnp.sum(bc_sum, 1).transpose(1, 0, 2).reshape(8, 12, 256)
    grad_w_bc = lax.dynamic_index_in_dim(bc_sum, mp, 0, keepdims=False)
    g_kbc = lax.dynamic_index_in_dim(sums[0:10].reshape(5, 128, 2), everyone, 1, keepdims=False)
    g_gain = lax.dynamic_index_in_dim(sums[10:22].reshape(128, 12), everyone, 0, keepdims=False)
    chans = lax.dynamic_index_in_dim(sums[24:66].reshape(7, 2, half), xl, 1, keepdims=False)
    own = lax.dynamic_index_in_dim(chans.reshape(7, 16, half // 16), dp, 1, keepdims=False)
    per_head = jnp.sum(chans[6].reshape(own_heads, -1), 1)
    head_rows = lax.dynamic_index_in_dim(sums[66:68, :heads].reshape(2, 2, own_heads), xl, 1, keepdims=False)

    gain_in = small[IN_GAIN : IN_GAIN + 12].reshape(model)
    h = hidden.astype(F32)
    inv_own = lax.rsqrt(jnp.mean(h * h, -1, keepdims=True) + EPS)
    hat = grad_normed * gain_in
    grad_hidden = (
        cotangent.astype(F32)
        + inv_own * hat
        - h * (inv_own * inv_own * inv_own) * jnp.mean(hat * h, -1, keepdims=True)
    )
    return (
        mixed,
        grad_hidden,
        g_gain,
        zo_sum[0],
        xe_sum[:, :half],
        xe_sum[:, half + 128 : half + 128 + own_heads],
        grad_w_bc,
        own[0:4],
        own[4],
        g_kbc[0:4],
        g_kbc[4],
        head_rows[0],
        per_head,
        head_rows[1],
        own[5],
        zo_sum[1].T,
    )


def solution(mesh):
    in_specs = (
        P("dp", "mp", None),
        P("dp", None),
        P("dp", "mp", None),
        P(("dp", "mp")),
        P("dp", "mp"),
        P("dp", "mp"),
        P("dp", "mp"),
        P(("dp", "mp"), None),
        P(None, ("mp", "dp")),
        P(("mp", "dp")),
        P(None, ("dp", "mp")),
        P(("dp", "mp")),
        P("mp"),
        P("mp"),
        P("mp"),
        P(("mp", "dp")),
        P("mp", "dp"),
    )
    out_specs = (
        P("dp", "mp", None),
        P("dp", "mp", None),
        P(("dp", "mp")),
        P("dp", "mp"),
        P("dp", "mp"),
        P("dp", "mp"),
        P(("dp", "mp"), None),
        P(None, ("mp", "dp")),
        P(("mp", "dp")),
        P(None, ("dp", "mp")),
        P(("dp", "mp")),
        P("mp"),
        P("mp"),
        P("mp"),
        P(("mp", "dp")),
        P("mp", "dp"),
    )
    return jax.shard_map(local, mesh=mesh, in_specs=in_specs, out_specs=out_specs, check_vma=False)
```

```python
import jax
import jax.numpy as jnp
from jax import lax
from jax.experimental import pallas as pl
from jax.experimental.pallas import tpu as pltpu
from jax.sharding import PartitionSpec as P

MESH = pl.DeviceIdType.MESH
EPS = 1e-05
Q = 128
HALO = 8
F32 = jnp.float32
BF16 = jnp.bfloat16
LOG2E = 1.4426950408889634
VMEM_LIMIT = 60 * 1024 * 1024

KEEP = 0
AHEAD = 4
SEG, ENTER, LEAVE, CARRY, SCALE, COEF = 8, 9, 10, 11, 12, 13
STEP_ROWS = 256

BC_TAPS, IN_GAIN, X_TAPS, HEAD_ROWS, SMALL_SHARED, SMALL_ROWS = 0, 10, 24, 60, 24, 64


def dot(a, b, dims=((1,), (0,))):
    return lax.dot_general(a, b, (dims, ((), ())), preferred_element_type=F32)


def dot_exact(a, b, dims=((1,), (0,))):
    return lax.dot_general(
        a, b, (dims, ((), ())), preferred_element_type=F32, precision=lax.Precision.HIGHEST
    )


NT = ((1,), (1,))
TN = ((0,), (0,))


def sigmoid(v):
    return 1.0 / (1.0 + jnp.exp(-v))


def softplus(v):
    return jnp.maximum(v, 0.0) + jnp.log1p(jnp.exp(-jnp.abs(v)))


def wide(small, row, count):
    return jnp.concatenate([small[row + i : row + i + 1] for i in range(count)], 1)


def columns_of(rows16):
    return jnp.concatenate([rows16, jnp.zeros((128 - rows16.shape[0], Q), F32)], 0).T


def lanes_of(tok, lane):
    return tok[:, lane : lane + 1]


def expand(values, width):
    rows = values.shape[0]
    first = lax.broadcasted_iota(jnp.int32, (rows, 128), 1) < 64
    pieces = []
    for pair in range(width // 128):
        a = jnp.broadcast_to(values[:, 2 * pair : 2 * pair + 1], (rows, 128))
        b = jnp.broadcast_to(values[:, 2 * pair + 1 : 2 * pair + 2], (rows, 128))
        pieces.append(jnp.where(first, a, b))
    return jnp.concatenate(pieces, 1)


def head_sums(values):
    width = values.shape[1]
    channel = lax.broadcasted_iota(jnp.int32, (width, 128), 0)
    lane = lax.broadcasted_iota(jnp.int32, (width, 128), 1)
    pick = jnp.where((channel >= lane * 64) & (channel < lane * 64 + 64), 1.0, 0.0).astype(BF16)
    high = values.astype(BF16)
    low = (values - high.astype(F32)).astype(BF16)
    return dot(high, pick) + dot(low, pick)


def rows8(values):
    total = values[0:8]
    for start in range(8, values.shape[0], 8):
        total = total + values[start : start + 8]
    return total


def causal():
    row = lax.broadcasted_iota(jnp.int32, (Q, Q), 0)
    col = lax.broadcasted_iota(jnp.int32, (Q, Q), 1)
    return row >= col


def pair_blocks(values):
    first = lax.broadcasted_iota(jnp.int32, values.shape, 1) < 64
    zero = jnp.zeros_like(values)
    return jnp.concatenate([jnp.where(first, values, zero), jnp.where(first, zero, values)], 0)


def decays(dt, hp, tok):
    step = softplus(dt + hp[2:3])
    rate = -jnp.exp(hp[0:1]) * step
    tri = jnp.where(causal(), 1.0, 0.0)
    cum = dot_exact(tri, rate)
    last = cum[Q - 1 : Q]
    enter = jnp.exp(cum) * lanes_of(tok, ENTER)
    leave = jnp.exp(last - cum) * lanes_of(tok, LEAVE)
    keep = jnp.exp(last) * tok[0:1, CARRY : CARRY + 1]
    cum2 = cum * LOG2E
    return step, rate, cum2, cum2.T, enter, leave, keep


def gaps(cum2, cum2_t, head):
    return jnp.exp2(jnp.minimum(cum2[:, head : head + 1] - cum2_t[head : head + 1, :], 0.0))


def place():
    dp, mp = lax.axis_index("dp"), lax.axis_index("mp")
    return {"xh": dp // 8, "z": (dp // 2) % 4, "c": dp % 2, "y": mp // 2, "xl": mp % 2}


def device(at, **other):
    at = {**at, **other}
    return (at["xh"] * 8 + at["z"] * 2 + at["c"], at["y"] * 2 + at["xl"])


def group_peers(at):
    peers = []
    for dy in range(4):
        for flip in range(2):
            if dy or flip:
                peers.append({**at, "y": (at["y"] + dy) % 4, "xl": (at["xl"] + flip) % 2})
    return peers


def x_peers(at):
    flips = [(0, 1), (1, 0), (1, 1)]
    return [{**at, "xh": (at["xh"] + a) % 2, "xl": (at["xl"] + b) % 2} for a, b in flips]


def z_peers(at):
    return [{**at, "z": (at["z"] + d) % 4} for d in range(1, 4)]


def y_peers(at):
    return [{**at, "y": (at["y"] + d) % 4} for d in range(1, 4)]


def core_peers(at):
    return [{**at, "c": 1 - at["c"]}]


def greet_begin(peers):
    barrier = pltpu.get_barrier_semaphore()
    for peer in peers:
        pl.semaphore_signal(barrier, inc=1, device_id=device(peer), device_id_type=MESH)


def greet_end(peers):
    pl.semaphore_wait(pltpu.get_barrier_semaphore(), len(peers))


def greet(peers):
    greet_begin(peers)
    greet_end(peers)


class Sends:
    def __init__(self, send_sems, recv_sems):
        self.send_sems, self.recv_sems, self.used = send_sems, recv_sems, 0

    def make(self, source, target, peer):
        slot = self.used
        self.used += 1
        return pltpu.make_async_remote_copy(
            src_ref=source,
            dst_ref=target,
            send_sem=self.send_sems.at[slot],
            recv_sem=self.recv_sems.at[slot],
            device_id=device(peer),
            device_id_type=MESH,
        )

    def start(self, source, target, peer):
        copy = self.make(source, target, peer)
        copy.start()
        return copy


def start_all(copies):
    for copy in copies:
        copy.start()


def wait_all(copies):
    for copy in copies:
        copy.wait()


def here_copies(pairs, sems):
    copies = [pltpu.make_async_copy(a, b, sems.at[i]) for i, (a, b) in enumerate(pairs)]
    start_all(copies)
    return copies


class Exchange:
    def __init__(self, total, taken, peers, held, sends):
        self.total, self.taken, self.held, self.count = total, taken, held, len(peers)
        rows = pl.ds(0, taken)
        self.copies = [sends.start(total.at[rows], held.at[i, rows], peer) for i, peer in enumerate(peers)]

    def finish(self):
        wait_all(self.copies)
        add = self.total[0 : self.taken]
        for i in range(self.count):
            add = add + self.held[i, 0 : self.taken]
        self.total[0 : self.taken] = add


def exchange(total, taken, peers, held, sends):
    Exchange(total, taken, peers, held, sends).finish()


class RingGather:
    SEMS = 7

    def __init__(self, at, source, target, send_sems, recv_sems, local_sem):
        self.at, self.source, self.target = at, source, target
        self.sems = (send_sems, recv_sems)
        self.local_sem = local_sem
        self.up, self.down = {**at, "y": (at["y"] + 1) % 4}, {**at, "y": (at["y"] + 3) % 4}
        self.pair = {**at, "xl": 1 - at["xl"]}

    def rows(self, y, xl):
        return self.target.at[pl.ds(pl.multiple_of((y * 2 + xl) * Q, Q), Q)]

    def copies(self, stage):
        at = self.at
        y, xl, other = at["y"], at["xl"], 1 - at["xl"]
        sends = Sends(*self.sems)
        if stage == 0:
            mine = self.rows(y, xl)
            own = self.source.at[xl]
            return [sends.make(self.source.at[other], mine, self.pair)] + [
                sends.make(own, mine, p) for p in (self.up, self.down)
            ]
        if stage == 1:
            sends.used = 3
            got = self.rows(y, other)
            return [sends.make(got, got, p) for p in (self.up, self.down)]
        sends.used = 5
        low, high = self.rows((y + 3) % 4, xl), self.rows((y + 1) % 4, other)
        return [sends.make(low, low, self.up), sends.make(high, high, self.down)]

    def local(self):
        return pltpu.make_async_copy(self.source.at[self.at["xl"]], self.rows(self.at["y"], self.at["xl"]), self.local_sem)

    def begin(self):
        start_all(self.copies(0))
        self.local().start()

    def second(self):
        self.copies(0)[0].wait()
        start_all(self.copies(1))

    def third(self):
        wait_all(self.copies(0)[1:])
        wait_all(self.copies(1))
        start_all(self.copies(2))

    def finish(self):
        wait_all(self.copies(2))
        self.local().wait()


class RingScatter:
    SEMS = 7

    @staticmethod
    def scratch(width):
        return [pltpu.VMEM((8, Q, width), BF16), dma(RingScatter.SEMS), dma(RingScatter.SEMS)]

    def __init__(self, at, part, refs):
        self.at, self.part = at, part
        self.held, self.ss, self.rs = refs
        y = at["y"]
        self.up_y, self.down_y, self.far_y = (y + 1) % 4, (y + 3) % 4, (y + 2) % 4
        self.up, self.down = {**at, "y": self.up_y}, {**at, "y": self.down_y}
        self.pair = {**at, "xl": 1 - at["xl"]}

    def copy(self, number):
        sends = Sends(self.ss, self.rs)
        sends.used = number
        if number == 6:
            return sends.make(self.held.at[6], self.held.at[7], self.pair)
        y, x = [(self.far_y, 0), (self.far_y, 1), (self.up_y, 1), (self.down_y, 0), (self.up_y, 0), (self.down_y, 1)][number]
        peer = self.down if number % 2 else self.up
        return sends.make(self.part.at[y * 2 + x], self.held.at[number], peer)

    def send_far(self):
        start_all([self.copy(0), self.copy(1)])

    def send_up(self):
        self.copy(2).start()

    def send_down(self):
        self.copy(3).start()

    def second(self):
        wait_all([self.copy(0), self.copy(1)])
        for slot, number in ((self.up_y * 2, 0), (self.down_y * 2 + 1, 1)):
            self.part[slot] = (self.part[slot].astype(F32) + self.held[number].astype(F32)).astype(BF16)
        start_all([self.copy(4), self.copy(5)])

    def third(self, out):
        wait_all([self.copy(n) for n in range(2, 6)])
        held, xl, y = self.held, self.at["xl"], self.at["y"]
        totals = []
        for x in range(2):
            totals.append(self.part[y * 2 + x].astype(F32) + held[3 - x].astype(F32) + held[4 + x].astype(F32))
        out[xl] = jnp.where(xl == 0, totals[0], totals[1]).astype(BF16)
        held[6] = jnp.where(xl == 0, totals[1], totals[0]).astype(BF16)
        self.copy(6).start()

    def finish(self, out):
        self.copy(6).wait()
        out[1 - self.at["xl"]] = self.held[7]


def ring_greets(at):
    return [{**at, "y": (at["y"] + 1) % 4}, {**at, "y": (at["y"] + 3) % 4}, {**at, "xl": 1 - at["xl"]}]


class PlaneGather:
    SEMS = 31

    def __init__(self, at, source, target, send_sems, recv_sems, local_sem, start=0, count=None):
        self.at, self.source, self.target = at, source, target
        self.sems, self.local_sem = (send_sems, recv_sems), local_sem
        depth, part = source.shape[1], source.shape[2]
        self.whole = count is None
        self.start, self.count = start, part if self.whole else count
        self.part = part
        self.upper, self.lower = pl.ds(0, depth // 2), pl.ds(depth // 2, depth // 2)
        self.lanes = pl.ds(self.start, self.count)
        self.cols = pl.ds(pl.multiple_of(at["xl"] * part + self.start, 128), self.count)
        self.both = [pl.ds(0, 2 * part)] if self.whole else [pl.ds(n * part + start, count) for n in range(2)]

    def copies(self, stage):
        at, w = self.at, self.target
        xh, z, c = at["xh"], at["z"], at["c"]
        sends = Sends(*self.sems)
        if stage == 0:
            return [
                sends.make(self.source.at[:, self.upper, self.lanes], w.at[:, xh, z, c, self.upper, self.cols], p)
                for p in x_peers(at)
            ] + [
                sends.make(self.source.at[:, self.lower, self.lanes], w.at[:, xh, z, c, self.lower, self.cols], p)
                for p in z_peers(at)
            ]
        if stage == 1:
            sends.used = 6
            copies = []
            for p in z_peers(at):
                for cols in self.both:
                    up = w.at[:, :, z, c, self.upper, cols]
                    copies.append(sends.make(up, up, p))
            low = w.at[:, xh, :, c, self.lower, self.cols]
            return copies + [sends.make(low, low, p) for p in x_peers(at)]
        sends.used = 15
        copies = []
        for cols in self.both:
            if self.count == 128:
                slots = [w.at[:, :, :, c, :, cols]]
            else:
                slots = [w.at[:, a, b, c, :, cols] for a in range(2) for b in range(4)]
            copies += [sends.make(slot, slot, core_peers(at)[0]) for slot in slots]
        return copies

    def local(self):
        at = self.at
        return pltpu.make_async_copy(
            self.source.at[:, :, self.lanes],
            self.target.at[:, at["xh"], at["z"], at["c"], :, self.cols],
            self.local_sem,
        )

    def begin(self):
        start_all(self.copies(0))
        self.local().start()

    def second(self):
        self.local().wait()
        wait_all(self.copies(0))
        start_all(self.copies(1))

    def third(self):
        wait_all(self.copies(1))
        start_all(self.copies(2))

    def finish(self):
        wait_all(self.copies(2))


class Layout:
    def __init__(self, width):
        self.width, self.half = width, width // 2
        self.part = self.half + 256
        self.total = 2 * self.part
        self.dt_at, self.bc_at = self.half, self.half + 128

    def x(self, v):
        return jnp.concatenate([v[:, : self.half], v[:, self.part : self.part + self.half]], 1)

    def bc(self, v):
        a, b = self.bc_at, self.part + self.bc_at
        return jnp.concatenate([v[:, a : a + 128], v[:, b : b + 128]], 1)

    def dt(self, v, own_heads):
        a, b = self.dt_at, self.part + self.dt_at
        return v[:, a : a + 128] + pltpu.roll(v[:, b : b + 128], own_heads, 1)

    def join(self, x, bc, dt, own_heads):
        lane = lax.broadcasted_iota(jnp.int32, dt.shape, 1)
        first = jnp.where(lane < own_heads, dt, 0.0)
        second = jnp.where(lane < own_heads, pltpu.roll(dt, 128 - own_heads, 1), 0.0)
        return jnp.concatenate(
            [x[:, : self.half], first, bc[:, :128], x[:, self.half :], second, bc[:, 128:]], 1
        )


def own_heads_of(width):
    return width // 128


def chunk_rows(j):
    return pl.ds(pl.multiple_of(j * Q, Q), Q)


def forward_kernel(
    tok_ref, small_ref, hid_ref, wxe_ref, cot_ref, w2_ref,
    zx_ref, xin_ref, bcin_ref, dt_ref, bcc_ref, y_ref, start_ref, gon_ref,
    normed_ref, cot_all_ref, w2_all_ref, stat_ref,
    state, xh, bch, xes, cots, weights, normeds, ys, stats, held,
    cot_send, cot_recv, w_send, w_recv, stat_send, stat_recv, sems,
):
    step = pl.program_id(0)
    steps = pl.num_programs(0) // 2
    per_step = STEP_ROWS // Q
    width = zx_ref.shape[2]
    lay = Layout(width)
    pairs = width // 128
    chunks = stats.shape[0] // 2
    own_heads = own_heads_of(width)
    at = place()
    ring = RingGather(at, cot_ref, cots, cot_send, cot_recv, sems.at[0])
    plane = PlaneGather(at, w2_ref, weights, w_send, w_recv, sems.at[1])

    def results():
        pairs_of = [(cots, cot_all_ref), (weights, w2_all_ref), (normeds, normed_ref)]
        return [pltpu.make_async_copy(a, b, sems.at[2 + i]) for i, (a, b) in enumerate(pairs_of)]

    @pl.when(step == 0)
    def _():
        greet(ring_greets(at) + y_peers(at)[1:2] + plane_greets(at))
        ring.begin()
        plane.begin()
        state[...] = jnp.zeros_like(state)
        xh[0:HALO] = jnp.zeros((HALO, width), F32)
        bch[0:HALO] = jnp.zeros((HALO, bch.shape[1]), F32)

    @pl.when(step == 1)
    def _():
        ring.second()
        plane.second()

    @pl.when(step == 2)
    def _():
        ring.third()

    @pl.when(step == 3)
    def _():
        plane.third()

    @pl.when(step == steps)
    def _():
        ring.finish()
        plane.finish()
        start_all(results())

    @pl.when(step < steps)
    def _():
        rows = hid_ref[...].astype(F32)
        inv_rms = lax.rsqrt(jnp.mean(rows * rows, -1, keepdims=True) + EPS)
        normed = (rows * inv_rms * wide(small_ref, IN_GAIN, 12)).astype(BF16)
        normeds[pl.ds(pl.multiple_of(step * STEP_ROWS, STEP_ROWS), STEP_ROWS)] = normed
        xes[...] = dot(normed, wxe_ref[...])

        @pl.loop(0, per_step)
        def _(j):
            chunk = step * per_step + j
            here = chunk_rows(j)

            @pl.when(chunk > 0)
            def _():
                xh[0:HALO] = xh[Q : Q + HALO]
                bch[0:HALO] = bch[Q : Q + HALO]

            rows16 = tok_ref[chunk]
            tok = columns_of(rows16)
            hp = small_ref[HEAD_ROWS : HEAD_ROWS + 3]
            xe = xes[here]
            x_in, bc_in, dt_in = lay.x(xe), lay.bc(xe), lay.dt(xe, own_heads)
            xin_ref[here] = x_in.astype(BF16)
            bcin_ref[here] = bc_in.astype(BF16)
            dt_ref[here] = dt_in

            def conv(held_rows, new, row, count):
                held_rows[HALO : HALO + Q] = new
                taps = [wide(small_ref, row + t * count, count) for t in range(5)]
                out = taps[4] + taps[3] * new
                for t in range(1, 4):
                    out = out + (taps[3 - t] * held_rows[HALO - t : HALO - t + Q]) * lanes_of(tok, KEEP + t)
                return out

            xc = conv(xh, x_in, X_TAPS, pairs)
            bcc = conv(bch, bc_in, BC_TAPS, 2)
            zx_ref[0, here] = xc
            bcc_ref[here] = bcc
            x_act = xc * sigmoid(xc)
            bc_act = bcc * sigmoid(bcc)
            n = bc_act.shape[1] // 2
            b_low = bc_act[:, :n].astype(BF16)
            c_low = bc_act[:, n:].astype(BF16)
            size, rate, cum2, cum2_t, enter, leave, keep = decays(dt_in, hp, tok)
            same = causal() & (lanes_of(tok, SEG) == rows16[SEG : SEG + 1])
            scores = jnp.where(same, dot(c_low, b_low, NT), 0.0)
            xs = x_act * expand(size, width)
            xs_low = xs.astype(BF16)
            before = state[...]
            before_low = before.astype(BF16)
            start_ref[j] = before_low
            inter = dot(c_low, before_low) * expand(enter, width)
            outs = []
            for pair in range(pairs):
                mixes = [(scores * gaps(cum2, cum2_t, 2 * pair + i)).astype(BF16) for i in range(2)]
                outs.append(
                    dot(jnp.concatenate(mixes, 1), pair_blocks(xs_low[:, pair * 128 : pair * 128 + 128]))
                )
            skip = expand(jnp.broadcast_to(hp[1:2], (8, 128)), width)[0:1]
            y = jnp.concatenate(outs, 1) + inter + skip * x_act
            y_ref[here] = y
            ys[chunk_rows(chunk)] = y
            moved = (xs * expand(leave, width)).astype(BF16)
            keep_all = expand(jnp.broadcast_to(keep, (8, 128)), width)[0:1]
            state[...] = before * keep_all + dot(b_low, moved, TN)

    @pl.when(step >= steps)
    def _():
        rows = pl.ds(pl.multiple_of((step - steps) * STEP_ROWS, STEP_ROWS), STEP_ROWS)
        full = weights.shape[1] * weights.shape[2] * weights.shape[3] * weights.shape[4]
        z = dot(normeds[rows], weights[0].reshape(full, width))
        gon = dot(cots[rows], weights[1].reshape(full, width))
        zx_ref[0] = z
        gon_ref[...] = gon.astype(BF16)
        gated = ys[rows] * (z * sigmoid(z))
        inner = gated * (gon * wide(small_ref, X_TAPS + 5 * pairs, pairs))
        for j in range(per_step):
            chunk = (step - steps) * per_step + j
            cut = slice(j * Q, j * Q + Q)
            stats[pl.ds(chunk, 1), :] = row_sums(gated[cut] * gated[cut])
            stats[pl.ds(chunks + chunk, 1), :] = row_sums(inner[cut])

    @pl.when(step == 2 * steps - 1)
    def _():
        wait_all(results())
        exchange(stats, stats.shape[0], y_peers(at), held, Sends(stat_send, stat_recv))
        inner = width * 4
        scale = lax.rsqrt(stats[0:chunks] / inner + EPS)
        stat_ref[0:chunks] = scale
        stat_ref[chunks : 2 * chunks] = scale * scale * scale * stats[chunks : 2 * chunks] / inner


def row_sums(values):
    total = values[:, 0:128]
    for start in range(128, values.shape[1], 128):
        total = total + values[:, start : start + 128]
    return jnp.sum(total.T, axis=0, keepdims=True)


def half_of(value, xl):
    half = value.shape[-1] // 2
    return jnp.where(xl == 0, value[..., :half], value[..., half:])


class PlaneSum:
    SEMS = 20

    @staticmethod
    def scratch(depth, width):
        cut, half = depth // 2, width // 2
        return [
            pltpu.VMEM((2, 4, depth, width), BF16),
            pltpu.VMEM((3, 4, cut, half), BF16),
            pltpu.VMEM((3, 2, cut, width), BF16),
            pltpu.VMEM((4, cut, half), BF16),
            pltpu.VMEM((2, cut, width), BF16),
            pltpu.VMEM((3, cut, half), BF16),
            pltpu.VMEM((3, cut, half), BF16),
            dma(PlaneSum.SEMS),
            dma(PlaneSum.SEMS),
        ]

    def __init__(self, at, source, refs):
        self.at, self.source = at, source
        (self.got, self.a2, self.b2, self.sa, self.sb, self.a3, self.b3, self.ss, self.rs) = refs
        self.depth, self.width = self.got.shape[2], self.got.shape[3]
        self.cut, self.half = self.depth // 2, self.width // 2

    def columns(self, xl):
        return pl.ds(pl.multiple_of(xl * self.half, 128), self.half)

    def sends(self, used):
        sends = Sends(self.ss, self.rs)
        sends.used = used
        return sends

    def first(self, far, z):
        peer, xh = core_peers(self.at)[0], (self.at["xh"] + far) % 2
        source = self.source.at[xh, z, peer["c"], :, pl.ds(0, self.width)]
        return self.sends((1 - far) * 4 + z).make(source, self.got.at[xh, z], peer)

    def second_x(self, number):
        p, c = x_peers(self.at)[number], self.at["c"]
        source = self.source.at[p["xh"], :, c, pl.ds(0, self.cut), self.columns(p["xl"])]
        return self.sends(8 + number).make(source, self.a2.at[number], p)

    def second_z(self, number):
        p, c = z_peers(self.at)[number], self.at["c"]
        source = self.source.at[:, p["z"], c, pl.ds(self.cut, self.cut), pl.ds(0, self.width)]
        return self.sends(11 + number).make(source, self.b2.at[number], p)

    def third(self):
        sends = self.sends(14)
        copies = []
        for i, p in enumerate(z_peers(self.at)):
            copies.append(sends.make(self.sa.at[p["z"]], self.a3.at[i], p))
        for i, p in enumerate(x_peers(self.at)):
            copies.append(sends.make(self.sb.at[p["xh"], :, self.columns(p["xl"])], self.b3.at[i], p))
        return copies

    def begin(self):
        start_all([self.first(far, z) for far in (1, 0) for z in range(4)])

    def after_cores(self):
        c = self.at["c"]
        for far in (1, 0):
            xh = (self.at["xh"] + far) % 2
            for z in range(4):
                self.first(far, z).wait()
                total = self.source[xh, z, c, :, 0 : self.width].astype(F32) + self.got[xh, z].astype(F32)
                self.source[xh, z, c, :, 0 : self.width] = total.astype(BF16)
            start_all([self.second_x(n) for n in ((1, 2) if far else (0,))])
        start_all([self.second_z(n) for n in range(3)])

    def after_first_axis(self):
        wait_all([self.second_x(n) for n in range(3)] + [self.second_z(n) for n in range(3)])
        at, cut, width = self.at, self.cut, self.width
        c = at["c"]

        @pl.loop(0, 4)
        def _(z):
            total = half_of(self.source[at["xh"], z, c, 0:cut, 0:width], at["xl"]).astype(F32)
            for i in range(3):
                total = total + self.a2[i, z].astype(F32)
            self.sa[z] = total.astype(BF16)

        for xh in range(2):
            total = self.source[xh, at["z"], c, cut : 2 * cut, 0:width].astype(F32)
            for i in range(3):
                total = total + self.b2[i, xh].astype(F32)
            self.sb[xh] = total.astype(BF16)
        start_all(self.third())

    def finish(self, out):
        wait_all(self.third())
        at, cut = self.at, self.cut
        total = self.sa[at["z"]].astype(F32)
        for i in range(3):
            total = total + self.a3[i].astype(F32)
        out[0:cut] = total
        total = half_of(self.sb[at["xh"]], at["xl"]).astype(F32)
        for i in range(3):
            total = total + self.b3[i].astype(F32)
        out[cut : 2 * cut] = total


def plane_greets(at):
    return x_peers(at)[1:] + z_peers(at) + core_peers(at)


PRE, MIX = 4, 4


def owner_block(step, y):
    return (y + jnp.where(step == 0, 2, jnp.where(step == 1, 1, jnp.where(step == 2, 3, 0)))) % 4


def block_rows(number):
    return pl.ds(pl.multiple_of(number * STEP_ROWS, STEP_ROWS), STEP_ROWS)


def backward_kernel(
    tok_ref, stat_ref, small_ref, zx_ref, gon_ref, y_ref, xin_ref, bcin_ref, dt_ref, bcc_ref, start_ref,
    cot_ref, normed_ref, w2_ref, wxe_ref,
    out_ref, back_ref, gzo_ref, gxe_ref, sums_ref, bcs_ref,
    adjoint, dh, dbh, gkx, gkbc, ghead, ggain, cots, normeds, weight, wxe, outs_low, z_low, dy_all, part, source,
    held, bc_got, small_send, small_recv, bc_send, bc_recv, sems, *refs,
):
    step = pl.program_id(0)
    per_step = STEP_ROWS // Q
    width = zx_ref.shape[2]
    pairs = width // 128
    own_heads = own_heads_of(width)
    lay = Layout(width)
    chunks = tok_ref.shape[0]
    model = cots.shape[1]
    at = place()
    ring_out = RingScatter(at, part, refs[0:3])
    ring_in = RingScatter(at, part, refs[3:6])
    plane_zo = PlaneSum(at, source, refs[6:15])
    plane_xe = PlaneSum(at, source, refs[15:24])
    peers = group_peers(at)
    loads = [
        pltpu.make_async_copy(a, b, sems.at[n])
        for n, (a, b) in enumerate(
            [(w2_ref.at[1], weight), (cot_ref, cots), (normed_ref, normeds), (wxe_ref, wxe), (w2_ref.at[0], weight)]
        )
    ]

    def put_part(owner, value):
        low = value.astype(BF16)
        for x in range(2):
            part[owner * 2 + x] = low[x * Q : x * Q + Q]

    def put_grad(values, start, half):
        for quarter in range(4):
            cut = slice(quarter * (model // 4), (quarter + 1) * (model // 4))
            value = dot(values[0][:, cut], values[1], TN).astype(BF16)
            value = value.reshape(2, 2, model // 16, value.shape[1])
            xh, z = quarter // 2, (quarter % 2) * 2
            for n in range(2):
                first = n * start[1] + start[0]
                source[xh, z : z + 2, :, :, first : first + half] = value[..., n * half : n * half + half]

    @pl.when(step == 0)
    def _():
        start_all(loads[:4])
        greet_begin(peers + plane_greets(at))
        adjoint[...] = jnp.zeros_like(adjoint)
        dh[...] = jnp.zeros_like(dh)
        dbh[...] = jnp.zeros_like(dbh)
        gkx[...] = jnp.zeros_like(gkx)
        gkbc[...] = jnp.zeros_like(gkbc)
        ghead[...] = jnp.zeros_like(ghead)
        ggain[...] = jnp.zeros_like(ggain)
        loads[0].wait()

    @pl.when(step < PRE)
    def _():
        owner = owner_block(step, at["y"])
        rows = block_rows(owner)
        columns = []
        for j in range(per_step):
            chunk = owner * per_step + j
            columns.append(
                columns_of(jnp.concatenate([stat_ref[pl.ds(chunk, 1), :], stat_ref[pl.ds(chunks + chunk, 1), :]], 0))
            )
        columns = jnp.concatenate(columns, 0)
        scale, coef = columns[:, 0:1], columns[:, 1:2]
        gain = wide(small_ref, X_TAPS + 5 * pairs, pairs)
        z, y, gon = zx_ref[0], y_ref[...], gon_ref[...].astype(F32)
        z_sig = sigmoid(z)
        z_act = z * z_sig
        gated = y * z_act
        scaled = gated * scale
        out_low = (scaled * gain).astype(BF16)
        outs_low[rows] = out_low
        gkx[5] += rows8(gon * scaled)
        grad_gated = scale * (gon * gain) - gated * coef
        dy_all[rows] = (grad_gated * z_act).astype(BF16)
        z_low[rows] = (grad_gated * y * (z_sig * (1.0 + z * (1.0 - z_sig)))).astype(BF16)
        put_part(owner, dot(out_low, weight[...], NT))

    @pl.when(step == 0)
    def _():
        greet_end(peers + plane_greets(at))
        ring_out.send_far()

    @pl.when(step == 1)
    def _():
        ring_out.send_up()

    @pl.when(step == 2)
    def _():
        ring_out.send_down()

    @pl.when(step == PRE)
    def _():
        loads[4].start()
        loads[1].wait()
        loads[2].wait()
        half = width // 2
        put_grad((cots, outs_low[...]), (half, width), half)
        put_grad((normeds, z_low[...]), (0, width), half)
        plane_zo.begin()
        ring_out.second()

    @pl.when(step == PRE + 1)
    def _():
        plane_zo.after_cores()

    @pl.when(step == PRE + 2)
    def _():
        ring_out.third(out_ref)

    @pl.when(step == PRE + MIX - 1)
    def _():
        plane_zo.after_first_axis()
        ring_out.finish(out_ref)

    @pl.when((step >= PRE) & (step < PRE + MIX))
    def _():
        @pl.loop(0, per_step)
        def _(turn_in):
            j = per_step - 1 - turn_in
            chunk = (PRE + MIX - 1 - step) * per_step + j
            here = chunk_rows(j)
            there = chunk_rows(chunk)

            @pl.when(chunk < chunks - 1)
            def _():
                dh[Q : Q + HALO] = dh[0:HALO]
                dbh[Q : Q + HALO] = dbh[0:HALO]

            rows16 = tok_ref[chunk]
            tok = columns_of(rows16)
            hp = small_ref[HEAD_ROWS : HEAD_ROWS + 3]
            dt_in = dt_ref[here]
            xc = zx_ref[0, here]
            bcc = bcc_ref[here]
            x_sig = sigmoid(xc)
            x_act = xc * x_sig
            bc_sig = sigmoid(bcc)
            bc_act = bcc * bc_sig
            n = bc_act.shape[1] // 2
            b_low = bc_act[:, :n].astype(BF16)
            c_low = bc_act[:, n:].astype(BF16)
            size, rate, cum2, cum2_t, enter, leave, keep = decays(dt_in, hp, tok)
            same = causal() & (lanes_of(tok, SEG) == rows16[SEG : SEG + 1])
            scores = jnp.where(same, dot(c_low, b_low, NT), 0.0)
            step_all = expand(size, width)
            leave_all = expand(leave, width)
            xs = x_act * step_all
            xs_low = xs.astype(BF16)
            moved = (xs * leave_all).astype(BF16)
            dy_low = dy_all[there]
            dy = dy_low.astype(F32)
            dy_in = (dy * expand(enter, width)).astype(BF16)

            skip = expand(jnp.broadcast_to(hp[1:2], (8, 128)), width)[0:1]
            before_low = start_ref[j]
            after = adjoint[...]
            after_low = after.astype(BF16)

            from_state = dot(b_low, after_low)
            outs = []
            dscores = jnp.zeros((Q, Q), F32)
            for pair in range(pairs):
                cut = slice(pair * 128, pair * 128 + 128)
                dys = pair_blocks(dy_low[:, cut])
                inner = dot(dys, xs_low[:, cut], NT)
                mixes = []
                for i in range(2):
                    gap = gaps(cum2, cum2_t, 2 * pair + i)
                    mixes.append((scores * gap).astype(BF16))
                    dscores = dscores + inner[i * Q : i * Q + Q] * gap
                outs.append(dot(jnp.concatenate(mixes, 0), dys, TN))
            intra = jnp.concatenate(outs, 1)
            dscores = jnp.where(same, dscores, 0.0).astype(BF16)

            dxs = intra + leave_all * from_state
            dx_act = dxs * step_all + skip * dy
            gkx[6] += rows8(dy * x_act)
            plus = head_sums(dy * (y_ref[here] - skip * x_act))
            through = moved.astype(F32) * from_state
            minus = head_sums(xs_low.astype(F32) * intra + through)
            direct = head_sums(dxs * x_act)
            keep_all = expand(jnp.broadcast_to(keep, (8, 128)), width)[0:1]
            at_end = rows8(through) + keep_all * rows8(after * before_low.astype(F32))
            at_end = jnp.sum(head_sums(at_end), axis=0, keepdims=True)
            last_row = lax.broadcasted_iota(jnp.int32, (Q, 128), 0) == Q - 1
            dcum = plus - minus + jnp.where(last_row, at_end, 0.0)
            tri = jnp.where(causal(), 1.0, 0.0)
            drate = dot_exact(tri, dcum, TN)
            dstep = direct - jnp.exp(hp[0:1]) * drate
            ddt = dstep * sigmoid(dt_in + hp[2:3])
            ghead[0] += rows8(drate * rate)
            ghead[1] += rows8(ddt)

            dc = dot(dscores, b_low) + dot(dy_in, before_low, NT)
            db = dot(dscores, c_low, TN) + dot(moved, after_low, NT)
            adjoint[...] = keep_all * after + dot(c_low, dy_in, TN)

            def conv_back(held_rows, grad, new, row, count, out):
                held_rows[0:Q] = grad
                taps = [wide(small_ref, row + t * count, count) for t in range(4)]
                total = taps[3] * grad
                out[3] += rows8(new * grad)
                out[4] += rows8(grad)
                for t in range(1, 4):
                    piece = held_rows[t : t + Q] * lanes_of(tok, AHEAD + t)
                    total = total + taps[3 - t] * piece
                    out[3 - t] += rows8(new * piece)
                return total

            dxc = dx_act * (x_sig * (1.0 + xc * (1.0 - x_sig)))
            dx_in = conv_back(dh, dxc, xin_ref[here].astype(F32), X_TAPS, pairs, gkx)
            dbcc = jnp.concatenate([db, dc], 1) * (bc_sig * (1.0 + bcc * (1.0 - bc_sig)))
            dbc_in = conv_back(dbh, dbcc, bcin_ref[here].astype(F32), BC_TAPS, 2, gkbc)
            cots[there, 0 : lay.total] = lay.join(dx_in, dbc_in, ddt, own_heads).astype(BF16)

    @pl.when(step == PRE + MIX)
    def _():
        plane_zo.finish(gzo_ref)
        loads[3].wait()
        loads[4].wait()

        def part_in(number):
            owner = (at["y"] + number) % 4
            rows = block_rows(owner)
            value = dot(z_low[rows], weight[...], NT) + dot(cots[rows, 0 : lay.total], wxe[...], NT)
            ggain[...] += rows8(value * normeds[rows].astype(F32))
            put_part(owner, value)

        part_in(2)
        ring_in.send_far()
        put_grad((normeds, cots[:, 0 : lay.total]), (0, lay.part), lay.part)
        plane_xe.begin()
        part_in(1)
        ring_in.send_up()
        part_in(3)
        ring_in.send_down()
        ring_in.second()
        plane_xe.after_cores()
        part_in(0)

        sums_ref[...] = jnp.zeros_like(sums_ref)
        for t in range(5):
            put_wide(sums_ref, 2 * t, jnp.sum(gkbc[t], axis=0, keepdims=True))
        put_wide(sums_ref, IN_GAIN, jnp.sum(ggain[...], axis=0, keepdims=True) / wide(small_ref, IN_GAIN, model // 128))
        for t in range(7):
            put_wide(sums_ref, X_TAPS + t * pairs, jnp.sum(gkx[t], axis=0, keepdims=True))
        for t in range(2):
            put_wide(sums_ref, X_TAPS + 7 * pairs + t, jnp.sum(ghead[t], axis=0, keepdims=True))
        steps = [core_peers(at), x_peers(at), z_peers(at), y_peers(at)]
        sends = Sends(small_send, small_recv)
        rows = sums_ref.shape[0]
        exchange(sums_ref, rows, steps[0], held.at[0], sends)
        exchange(sums_ref, rows, steps[1], held.at[1], sends)
        plane_xe.after_first_axis()
        exchange(sums_ref, rows, steps[2], held.at[2], sends)
        ring_in.third(back_ref)
        exchange(sums_ref, SMALL_SHARED, steps[3], held.at[3], sends)
        plane_xe.finish(gxe_ref)
        bc_got[at["xl"], at["y"]] = gxe_ref[:, lay.bc_at : lay.bc_at + 128]
        slot = bc_got.at[at["xl"], at["y"]]
        sends = Sends(bc_send, bc_recv)
        wait_all([sends.start(slot, slot, p) for p in peers])
        for n in range(2):
            bcs_ref[n] = jnp.sum(bc_got[n], axis=0)
        ring_in.finish(back_ref)


def put_wide(ref, row, value):
    for i in range(value.shape[1] // 128):
        ref[row + i : row + i + 1] = value[:, i * 128 : i * 128 + 128]


def gather_kernel(
    hid, ids_ref, wx_ref, wdt_ref, wbc_ref, gain_ref, kx_ref, kxb_ref, kbc_ref, kbcb_ref, og_ref, al_ref, ds_ref, db_ref,
    hid_all, wxe_all, small_all, tok_all,
    wxe, bc_got, bc_rows, held, lanes,
    hid_send, hid_recv, bc_send, bc_recv, w_send, w_recv, wbc_send, wbc_recv, small_send, small_recv, sems,
):
    at = place()
    peers = group_peers(at)
    y, xl = at["y"], at["xl"]
    depth, half = wx_ref.shape
    own_heads = wdt_ref.shape[0]
    ring = RingGather(at, hid, hid_all, hid_send, hid_recv, sems.at[0])
    plane = PlaneGather(at, wxe, wxe_all, w_send, w_recv, sems.at[1], 0, half + 128)
    plane_bc = PlaneGather(at, wxe, wxe_all, wbc_send, wbc_recv, sems.at[2], half + 128, 128)

    wxe[0, :, 0:half] = wx_ref[...]
    lanes[...] = jnp.zeros_like(lanes)
    lanes[0:own_heads, 0:depth] = wdt_ref[...].astype(F32)
    wxe[0, :, half : half + 128] = columns_of(lanes[:, 0:128])[0:depth].astype(BF16)
    lanes[...] = jnp.zeros_like(lanes)
    lanes[0:2, 0:4] = kbc_ref[...].astype(F32)
    taps_bc = columns_of(lanes[:, 0:128])[0:4, 0:2]
    bc_slot = bc_got.at[y * 2 + xl]
    bc_got[y * 2 + xl, 0:12] = wbc_ref[...].astype(F32)

    def placed(pieces, width, start):
        lanes[...] = jnp.zeros_like(lanes)
        row = 0
        for piece in pieces:
            count, size = piece.shape
            lanes[row : row + count, 0:size] = piece[...].astype(F32)
            row += count
        return pltpu.roll(lanes[:, 0:width], start, 1)

    dp = at["xh"] * 8 + at["z"] * 2 + at["c"]
    everyone = dp * 8 + y * 2 + xl
    small_all[...] = jnp.zeros_like(small_all)
    value = placed([taps_bc, kbcb_ref], 256, everyone * kbc_ref.shape[0])
    for t in range(5):
        put_wide(small_all, BC_TAPS + 2 * t, value[t : t + 1])
    value = placed([gain_ref], lanes.shape[1], everyone * gain_ref.shape[1])
    put_wide(small_all, IN_GAIN, value[0:1])
    value = placed([kx_ref, kxb_ref, og_ref], 2 * half, xl * half + dp * kx_ref.shape[1])
    for t in range(6):
        put_wide(small_all, X_TAPS + t * (half // 64), value[t : t + 1])
    value = placed([al_ref, ds_ref, db_ref], 128, xl * own_heads)
    small_all[HEAD_ROWS : HEAD_ROWS + 3] = jnp.where(dp == 0, value[0:3], 0.0)

    greet_begin(peers + plane_greets(at))
    token_info(ids_ref[xl], tok_all)
    greet_end(peers + plane_greets(at))
    sends = Sends(bc_send, bc_recv)
    bc_copies = [sends.start(bc_slot, bc_slot, p) for p in peers]
    small_sends = Sends(small_send, small_recv)
    small = Exchange(small_all, SMALL_SHARED, y_peers(at), held.at[0], small_sends)
    plane.begin()
    ring.begin()

    wait_all(bc_copies)
    for m in range(8):
        bc_rows[12 * m : 12 * m + 12] = bc_got[m, 0:12]
    wxe[0, :, half + 128 : half + 256] = half_of(bc_rows[...], xl).astype(BF16)
    plane_bc.begin()
    small.finish()
    small = Exchange(small_all, SMALL_ROWS, core_peers(at), held.at[1], small_sends)
    plane.second()
    small.finish()
    small = Exchange(small_all, SMALL_ROWS, x_peers(at), held.at[2], small_sends)
    plane_bc.second()
    ring.second()
    small.finish()
    small = Exchange(small_all, SMALL_ROWS, z_peers(at), held.at[3], small_sends)
    plane.third()
    plane_bc.third()
    ring.third()
    small.finish()
    plane.finish()
    plane_bc.finish()
    ring.finish()


def block(rows, w, index):
    return pl.BlockSpec((rows, w), lambda i: (index(i), 0))


def whole(shape):
    return pl.BlockSpec(shape, lambda i: (0,) * len(shape), pipeline_mode=pl.Buffered(1))


def whole_out(shape):
    return pl.BlockSpec(shape, lambda i: (0,) * len(shape))


ANY = pl.BlockSpec(memory_space=pl.ANY)
IN_VMEM = pl.BlockSpec(memory_space=pltpu.VMEM)


def like(shape, dtype):
    return jax.ShapeDtypeStruct(shape, dtype)


def dma(count):
    return pltpu.SemaphoreType.DMA((count,))


def remote_params(cid):
    return pltpu.CompilerParams(collective_id=cid, has_side_effects=True, vmem_limit_bytes=VMEM_LIMIT)


def gather_call(hidden, ids, w_x, w_dt, w_bc, small_args):
    _, rows, model = hidden.shape
    depth, half = w_x.shape
    part = half + 256
    args = [ids, w_x, w_dt, w_bc, *small_args]
    return pl.pallas_call(
        gather_kernel,
        in_specs=[ANY] + [IN_VMEM] * len(args),
        out_specs=[ANY, ANY, IN_VMEM, IN_VMEM],
        out_shape=[
            like((8 * rows, model), BF16),
            like((1, 2, 4, 2, depth, 2 * part), BF16),
            like((SMALL_ROWS, 128), F32),
            like((ids.shape[1], 16, Q), F32),
        ],
        scratch_shapes=[
            pltpu.VMEM((1, depth, part), BF16),
            pltpu.VMEM((8, 16, w_bc.shape[1]), F32),
            pltpu.VMEM((depth, w_bc.shape[1]), F32),
            pltpu.VMEM((4, 3, SMALL_ROWS, 128), F32),
            pltpu.VMEM((8, model), F32),
            dma(7), dma(7), dma(7), dma(7), dma(31), dma(31), dma(31), dma(31), dma(10), dma(10), dma(3),
        ],
        name="gather",
        compiler_params=remote_params(0),
    )(hidden, *args)


def forward_call(tok, small, hid_all, wxe, cotangent, w2):
    length, model = hid_all.shape
    total = wxe.shape[1]
    depth, half = w2.shape[1], w2.shape[2]
    width = 2 * half
    steps = length // STEP_ROWS
    chunks = length // Q

    def early(i):
        return jnp.minimum(i, steps - 1)

    def late(i):
        return jnp.maximum(i - steps, 0)

    return pl.pallas_call(
        forward_kernel,
        grid=(2 * steps,),
        in_specs=[whole(tok.shape), whole(small.shape), block(STEP_ROWS, model, early), whole(wxe.shape), ANY, ANY],
        out_specs=[pl.BlockSpec((1, STEP_ROWS, width), lambda i: (i // steps, i % steps, 0)),
                   block(STEP_ROWS, width, early), block(STEP_ROWS, 256, early),
                   block(STEP_ROWS, 128, early), block(STEP_ROWS, 256, early), block(STEP_ROWS, width, early),
                   pl.BlockSpec((STEP_ROWS // Q, 128, width), lambda i: (early(i), 0, 0)),
                   block(STEP_ROWS, width, late), ANY, ANY, ANY, whole_out((2 * chunks, Q))],
        out_shape=[
            like((2, length, width), F32), like((length, width), BF16), like((length, 256), BF16),
            like((length, 128), F32),
            like((length, 256), F32), like((length, width), F32), like((chunks, 128, width), BF16),
            like((length, width), BF16), like((length, model), BF16), like((length, model), BF16),
            like((2, 2, 4, 2, depth, width), BF16), like((2 * chunks, Q), F32),
        ],
        scratch_shapes=[
            pltpu.VMEM((128, width), F32),
            pltpu.VMEM((Q + HALO, width), F32),
            pltpu.VMEM((Q + HALO, 256), F32),
            pltpu.VMEM((STEP_ROWS, total), F32),
            pltpu.VMEM((length, model), BF16),
            pltpu.VMEM((2, 2, 4, 2, depth, width), BF16),
            pltpu.VMEM((length, model), BF16),
            pltpu.VMEM((length, width), F32),
            pltpu.VMEM((2 * chunks, Q), F32),
            pltpu.VMEM((3, 2 * chunks, Q), F32),
            dma(7), dma(7), dma(31), dma(31), dma(3), dma(3), dma(5),
        ],
        name="mix_forward",
        compiler_params=remote_params(1),
    )(tok, small, hid_all, wxe, cotangent, w2)


def backward_call(tok, stat, small, zx, gon, y, xin, bcin, dt, bcc, starts, cots, normed, w2, wxe):
    length, width = y.shape
    model, total = wxe.shape
    depth = model // 16
    steps = length // STEP_ROWS

    def both(i):
        first = owner_block(i, lax.axis_index("mp") // 2)
        return jnp.where(i < PRE, first, jnp.maximum(PRE + MIX - 1 - i, 0))

    def mix(i):
        return jnp.clip(PRE + MIX - 1 - i, 0, steps - 1)

    def pre(i):
        return owner_block(jnp.minimum(i, PRE - 1), lax.axis_index("mp") // 2)

    return pl.pallas_call(
        backward_kernel,
        grid=(PRE + MIX + 1,),
        in_specs=[whole(tok.shape), whole(stat.shape), whole(small.shape),
                  pl.BlockSpec((1, STEP_ROWS, width), lambda i: (jnp.where(i < PRE, 1, 0), both(i), 0)),
                  block(STEP_ROWS, width, pre), block(STEP_ROWS, width, both),
                  block(STEP_ROWS, width, mix), block(STEP_ROWS, 256, mix), block(STEP_ROWS, 128, mix),
                  block(STEP_ROWS, 256, mix),
                  pl.BlockSpec((STEP_ROWS // Q, 128, width), lambda i: (mix(i), 0, 0)), ANY, ANY, ANY, ANY],
        out_specs=[whole((2, Q, model)), whole((2, Q, model)), whole((depth, width)), whole((depth, total // 2)),
                   whole((72, 128)), whole((2, depth, 128))],
        out_shape=[
            like((2, Q, model), BF16), like((2, Q, model), BF16), like((depth, width), F32),
            like((depth, total // 2), F32), like((72, 128), F32), like((2, depth, 128), F32),
        ],
        scratch_shapes=[
            pltpu.VMEM((128, width), F32),
            pltpu.VMEM((Q + HALO, width), F32),
            pltpu.VMEM((Q + HALO, 256), F32),
            pltpu.VMEM((7, 8, width), F32),
            pltpu.VMEM((5, 8, 256), F32),
            pltpu.VMEM((2, 8, 128), F32),
            pltpu.VMEM((8, model), F32),
            pltpu.VMEM((length, model), BF16),
            pltpu.VMEM((length, model), BF16),
            pltpu.VMEM((model, width), BF16),
            pltpu.VMEM((model, total), BF16),
            pltpu.VMEM((length, width), BF16),
            pltpu.VMEM((length, width), BF16),
            pltpu.VMEM((length, width), BF16),
            pltpu.VMEM((8, Q, model), BF16),
            pltpu.VMEM((2, 4, 2, depth, 2 * width), BF16),
            pltpu.VMEM((4, 3, 72, 128), F32),
            pltpu.VMEM((2, 4, depth, 128), F32),
            dma(10), dma(10), dma(7), dma(7), dma(5),
            *RingScatter.scratch(model),
            *RingScatter.scratch(model),
            *PlaneSum.scratch(depth, 2 * width),
            *PlaneSum.scratch(depth, total),
        ],
        name="mix_backward",
        compiler_params=remote_params(2),
    )(tok, stat, small, zx, gon, y, xin, bcin, dt, bcc, starts, cots, normed, w2, wxe)


def token_info(ids, out):
    chunks = ids.shape[0]
    seg = ids.astype(F32)
    lane = lax.broadcasted_iota(jnp.int32, seg.shape, 1)
    row = lax.broadcasted_iota(jnp.int32, seg.shape, 0)

    def chunk_back(v):
        return jnp.where(row == 0, -1.0, pltpu.roll(v, 1, 0))

    def chunk_ahead(v):
        return jnp.where(row == chunks - 1, -1.0, pltpu.roll(v, chunks - 1, 0))

    def flag(mask):
        return jnp.where(mask, 1.0, 0.0)

    tail = jnp.broadcast_to(seg[:, Q - 1 :], seg.shape)
    last = chunk_back(tail)
    rows = {SEG: seg, ENTER: flag(seg == last), LEAVE: flag(seg == tail), CARRY: flag(tail == last)}
    for j in range(1, 4):
        turned = pltpu.roll(seg, j, 1)
        rows[KEEP + j] = flag(jnp.where(lane < j, chunk_back(turned), turned) == seg)
        turned = pltpu.roll(seg, Q - j, 1)
        rows[AHEAD + j] = flag(jnp.where(lane >= Q - j, chunk_ahead(turned), turned) == seg)
    out[...] = jnp.zeros_like(out)
    for number, value in rows.items():
        for chunk in range(chunks):
            out[chunk, number : number + 1] = value[chunk : chunk + 1]


def finish_kernel(
    hid, cot, got, back, small, gzo, gxe, sums, bcs,
    mixed, g_hid, g_gain, g_wz, g_wx, g_wdt, g_wbc, g_kx, g_kxb, g_kbc, g_kbcb, g_al, g_ds, g_db, g_og, g_wo,
):
    at = place()
    xl, mp = at["xl"], at["y"] * 2 + at["xl"]
    dp = at["xh"] * 8 + at["z"] * 2 + at["c"]
    everyone = dp * 8 + mp
    depth, half = g_wz.shape
    model = hid.shape[2]
    own_heads = g_al.shape[1]
    gain_in = wide(small, IN_GAIN, model // 128)
    for s in range(hid.shape[0]):
        h = hid[s].astype(F32)
        mixed[s] = (h + got[s].astype(F32)).astype(BF16)
        inv = lax.rsqrt(jnp.mean(h * h, -1, keepdims=True) + EPS)
        hat = back[s].astype(F32) * gain_in
        g_hid[s] = (
            cot[s].astype(F32) + inv * hat - h * ((inv * inv * inv) * jnp.mean(hat * h, -1, keepdims=True))
        )
    g_wz[...] = gzo[:, 0:half]
    g_wo[...] = gzo[:, half : 2 * half].T
    g_wx[...] = gxe[:, 0:half]
    g_wdt[...] = gxe[:, half : half + 128].T[0:own_heads]

    def cut(values, start, count):
        width = values.shape[1]
        return pltpu.roll(values, lax.rem(width - start, width), 1)[:, 0:count]

    def tall(row, count):
        return jnp.broadcast_to(wide(sums, row, count), (8, count * 128))

    pairs = half // 64
    g_gain[...] = cut(tall(IN_GAIN, model // 128), everyone * g_gain.shape[1], g_gain.shape[1])[0:1]
    rows = jnp.concatenate([wide(sums, X_TAPS + t * pairs, pairs) for t in range(7)] + [jnp.zeros((1, 2 * half), F32)], 0)
    own = cut(rows, xl * half + dp * g_kx.shape[1], g_kx.shape[1])
    g_kx[...] = own[0:4]
    g_kxb[...] = own[4:5]
    g_og[...] = own[5:6]
    per_head = head_sums(rows)
    g_ds[...] = cut(per_head, xl * own_heads, own_heads)[6:7]
    per_head = jnp.concatenate([sums[64:72]], 0)
    per_head = cut(per_head, xl * own_heads, own_heads)
    first = X_TAPS + 7 * pairs - 64
    g_al[...] = per_head[first : first + 1]
    g_db[...] = per_head[first + 1 : first + 2]
    rows = jnp.concatenate([wide(sums, BC_TAPS + 2 * t, 2) for t in range(5)] + [jnp.zeros((3, 256), F32)], 0)
    own = cut(rows, everyone * 2, 128)
    g_kbc[...] = jnp.concatenate([own, jnp.zeros((120, 128), F32)], 0).T[0:2, 0:4]
    g_kbcb[...] = own[4:5, 0:2]
    total = jnp.concatenate([bcs[0], bcs[1]], 1)
    g_wbc[...] = pltpu.roll(total, lax.rem(depth - mp * 12, depth), 0)[0:12]


def finish_call(hidden, cotangent, got, back, small, gzo, gxe, sums, bcs, own_heads):
    depth, half = gzo.shape[0], gzo.shape[1] // 2
    shapes = [
        (hidden.shape, BF16), (hidden.shape, F32), ((1, hidden.shape[2] // 128), F32), ((depth, half), F32),
        ((depth, half), F32), ((own_heads, depth), F32), ((12, 256), F32), ((4, half // 16), F32),
        ((1, half // 16), F32), ((2, 4), F32), ((1, 2), F32), ((1, own_heads), F32), ((1, own_heads), F32),
        ((1, own_heads), F32), ((1, half // 16), F32), ((half, depth), F32),
    ]
    return pl.pallas_call(
        finish_kernel,
        in_specs=[IN_VMEM] * 9,
        out_specs=[IN_VMEM] * len(shapes),
        out_shape=[like(*shape) for shape in shapes],
        name="finish",
        compiler_params=pltpu.CompilerParams(vmem_limit_bytes=VMEM_LIMIT),
    )(hidden, cotangent, got, back, small, gzo, gxe, sums, bcs)


def local(
    hidden, segments, cotangent, norm_gain, w_z, w_x, w_dt, w_bc, conv_x, conv_x_bias, conv_bc, conv_bc_bias,
    a_log, d_skip, dt_bias, out_gain, w_out,
):
    _, _, model = hidden.shape
    depth, half = w_z.shape
    width = 2 * half
    own_heads = a_log.shape[0]
    lay = Layout(width)

    small_args = [
        norm_gain[None], conv_x, conv_x_bias[None], conv_bc.T, conv_bc_bias[None], out_gain[None],
        a_log[None], d_skip[None], dt_bias[None],
    ]
    ids = segments.reshape(segments.shape[0], -1, Q)
    hid_all, wxe_all, small, tok = gather_call(hidden, ids, w_x, w_dt.T, w_bc, small_args)
    full_xe = wxe_all.reshape(model, lay.total)
    w2 = jnp.stack([w_z, w_out.T])
    zx, xin, bcin, dt, bcc, y_out, starts, gon, normed, cot_all, w2_all, stat = forward_call(
        tok, small, hid_all, full_xe, cotangent, w2
    )
    got_out, grad_normed, zo_sum, xe_sum, sums, bc_sum = backward_call(
        tok, stat, small, zx, gon, y_out, xin, bcin, dt, bcc, starts, cot_all, normed,
        w2_all.reshape(2, model, width), full_xe,
    )
    (
        mixed, g_hid, g_gain, g_wz, g_wx, g_wdt, g_wbc, g_kx, g_kxb, g_kbc, g_kbcb, g_al, g_ds, g_db, g_og, g_wo,
    ) = finish_call(hidden, cotangent, got_out, grad_normed, small, zo_sum, xe_sum, sums, bc_sum, own_heads)
    return (
        mixed, g_hid, g_gain[0], g_wz, g_wx, g_wdt.T, g_wbc, g_kx, g_kxb[0], g_kbc.T, g_kbcb[0], g_al[0], g_ds[0],
        g_db[0], g_og[0], g_wo,
    )


def solution(mesh):
    in_specs = (
        P("dp", "mp", None),
        P("dp", None),
        P("dp", "mp", None),
        P(("dp", "mp")),
        P("dp", "mp"),
        P("dp", "mp"),
        P("dp", "mp"),
        P(("dp", "mp"), None),
        P(None, ("mp", "dp")),
        P(("mp", "dp")),
        P(None, ("dp", "mp")),
        P(("dp", "mp")),
        P("mp"),
        P("mp"),
        P("mp"),
        P(("mp", "dp")),
        P("mp", "dp"),
    )
    out_specs = (
        P("dp", "mp", None),
        P("dp", "mp", None),
        P(("dp", "mp")),
        P("dp", "mp"),
        P("dp", "mp"),
        P("dp", "mp"),
        P(("dp", "mp"), None),
        P(None, ("mp", "dp")),
        P(("mp", "dp")),
        P(None, ("dp", "mp")),
        P(("dp", "mp")),
        P("mp"),
        P("mp"),
        P("mp"),
        P(("mp", "dp")),
        P("mp", "dp"),
    )
    return jax.shard_map(local, mesh=mesh, in_specs=in_specs, out_specs=out_specs, check_vma=False)
```

```python
import jax
import jax.numpy as jnp
from jax import lax
from jax.experimental import pallas as pl
from jax.experimental.pallas import tpu as pltpu
from jax.sharding import PartitionSpec as P

MESH = pl.DeviceIdType.MESH
EPS = 1e-05
Q = 128
HALO = 8
F32 = jnp.float32
BF16 = jnp.bfloat16
LOG2E = 1.4426950408889634
VMEM_LIMIT = 60 * 1024 * 1024

KEEP = 0
AHEAD = 4
SEG, ENTER, LEAVE, CARRY, SCALE, COEF = 8, 9, 10, 11, 12, 13
STEP_ROWS = 256

BC_TAPS, IN_GAIN, X_TAPS, HEAD_ROWS, SMALL_SHARED, SMALL_ROWS = 0, 10, 24, 60, 24, 64


def dot(a, b, dims=((1,), (0,))):
    return lax.dot_general(a, b, (dims, ((), ())), preferred_element_type=F32)


def dot_exact(a, b, dims=((1,), (0,))):
    return lax.dot_general(
        a, b, (dims, ((), ())), preferred_element_type=F32, precision=lax.Precision.HIGHEST
    )


NT = ((1,), (1,))
TN = ((0,), (0,))


def sigmoid(v):
    return 0.5 + 0.5 * jnp.tanh(0.5 * v)


def softplus(v):
    return jnp.maximum(v, 0.0) + jnp.log1p(jnp.exp(-jnp.abs(v)))


def wide(small, row, count):
    return jnp.concatenate([small[row + i : row + i + 1] for i in range(count)], 1)


def columns_of(rows16):
    return jnp.concatenate([rows16, jnp.zeros((128 - rows16.shape[0], Q), F32)], 0).T


def lanes_of(tok, lane):
    return tok[:, lane : lane + 1]


def head_pick(width):
    channel = lax.broadcasted_iota(jnp.int32, (width, 128), 0)
    lane = lax.broadcasted_iota(jnp.int32, (width, 128), 1)
    return jnp.where((channel >= lane * 64) & (channel < lane * 64 + 64), 1.0, 0.0).astype(BF16)


def two_parts(values):
    high = values.astype(BF16)
    return high, (values - high.astype(F32)).astype(BF16)


def expand(values, pick):
    high, low = two_parts(values)
    return dot(high, pick, NT) + dot(low, pick, NT)


def head_sums(values, pick):
    high, low = two_parts(values)
    return dot(high, pick) + dot(low, pick)


def rows8(values):
    total = values[0:8]
    for start in range(8, values.shape[0], 8):
        total = total + values[start : start + 8]
    return total


def causal():
    row = lax.broadcasted_iota(jnp.int32, (Q, Q), 0)
    col = lax.broadcasted_iota(jnp.int32, (Q, Q), 1)
    return row >= col


def pair_blocks(values):
    first = lax.broadcasted_iota(jnp.int32, values.shape, 1) < 64
    zero = jnp.zeros_like(values)
    return jnp.concatenate([jnp.where(first, values, zero), jnp.where(first, zero, values)], 0)


def decays(dt, hp, tok):
    step = softplus(dt + hp[2:3])
    rate = -jnp.exp(hp[0:1]) * step
    tri = jnp.where(causal(), 1.0, 0.0)
    cum = dot_exact(tri, rate)
    last = cum[Q - 1 : Q]
    enter = jnp.exp(cum) * lanes_of(tok, ENTER)
    leave = jnp.exp(last - cum) * lanes_of(tok, LEAVE)
    keep = jnp.exp(last) * tok[0:1, CARRY : CARRY + 1]
    cum2 = cum * LOG2E
    return step, rate, cum2, cum2.T, enter, leave, keep


def gaps(cum2, cum2_t, head):
    return jnp.exp2(jnp.minimum(cum2[:, head : head + 1] - cum2_t[head : head + 1, :], 0.0))


def place():
    dp, mp = lax.axis_index("dp"), lax.axis_index("mp")
    return {"xh": dp // 8, "z": (dp // 2) % 4, "c": dp % 2, "y": mp // 2, "xl": mp % 2}


def device(at, **other):
    at = {**at, **other}
    return (at["xh"] * 8 + at["z"] * 2 + at["c"], at["y"] * 2 + at["xl"])


def group_peers(at):
    peers = []
    for dy in range(4):
        for flip in range(2):
            if dy or flip:
                peers.append({**at, "y": (at["y"] + dy) % 4, "xl": (at["xl"] + flip) % 2})
    return peers


def x_peers(at):
    flips = [(0, 1), (1, 0), (1, 1)]
    return [{**at, "xh": (at["xh"] + a) % 2, "xl": (at["xl"] + b) % 2} for a, b in flips]


def z_peers(at):
    return [{**at, "z": (at["z"] + d) % 4} for d in range(1, 4)]


def y_peers(at):
    return [{**at, "y": (at["y"] + d) % 4} for d in range(1, 4)]


def y_core_peers(at):
    return core_peers(at) + [{**p, "c": (at["c"] + flip) % 2} for flip in range(2) for p in y_peers(at)]


def core_peers(at):
    return [{**at, "c": 1 - at["c"]}]


def greet_begin(peers):
    barrier = pltpu.get_barrier_semaphore()
    for peer in peers:
        pl.semaphore_signal(barrier, inc=1, device_id=device(peer), device_id_type=MESH)


def greet_end(peers):
    pl.semaphore_wait(pltpu.get_barrier_semaphore(), len(peers))


def greet(peers):
    greet_begin(peers)
    greet_end(peers)


class Sends:
    def __init__(self, send_sems, recv_sems):
        self.send_sems, self.recv_sems, self.used = send_sems, recv_sems, 0

    def make(self, source, target, peer):
        slot = self.used
        self.used += 1
        return pltpu.make_async_remote_copy(
            src_ref=source,
            dst_ref=target,
            send_sem=self.send_sems.at[slot],
            recv_sem=self.recv_sems.at[slot],
            device_id=device(peer),
            device_id_type=MESH,
        )

    def start(self, source, target, peer):
        copy = self.make(source, target, peer)
        copy.start()
        return copy


def start_all(copies):
    for copy in copies:
        copy.start()


def wait_all(copies):
    for copy in copies:
        copy.wait()


def here_copies(pairs, sems):
    copies = [pltpu.make_async_copy(a, b, sems.at[i]) for i, (a, b) in enumerate(pairs)]
    start_all(copies)
    return copies


class Exchange:
    def __init__(self, total, taken, peers, held, sends):
        self.total, self.taken, self.held, self.count = total, taken, held, len(peers)
        rows = pl.ds(0, taken)
        self.copies = [sends.start(total.at[rows], held.at[i, rows], peer) for i, peer in enumerate(peers)]

    def finish(self):
        wait_all(self.copies)
        add = self.total[0 : self.taken]
        for i in range(self.count):
            add = add + self.held[i, 0 : self.taken]
        self.total[0 : self.taken] = add


def exchange(total, taken, peers, held, sends):
    Exchange(total, taken, peers, held, sends).finish()


PIECES = 2


def pieces():
    rows = Q // PIECES
    return [pl.ds(i * rows, rows) for i in range(PIECES)]


class YCoreExchange:
    def __init__(self, at, total, held, sends):
        self.total, self.held = total, held
        self.copies = [sends.start(total, held.at[i], peer) for i, peer in enumerate(y_core_peers(at))]

    def finish(self):
        wait_all(self.copies)
        shared = self.total[0:SMALL_SHARED]
        for i in range(len(self.copies)):
            shared = shared + self.held[i, 0:SMALL_SHARED]
        rows = slice(SMALL_SHARED, self.total.shape[0])
        self.total[rows] = self.total[rows] + self.held[0, rows]
        self.total[0:SMALL_SHARED] = shared


class RingGather:
    SEMS = 7 * PIECES

    def __init__(self, at, source, target, send_sems, recv_sems, local_sem):
        self.at, self.source, self.target = at, source, target
        self.sems = (send_sems, recv_sems)
        self.local_sem = local_sem
        self.up, self.down = {**at, "y": (at["y"] + 1) % 4}, {**at, "y": (at["y"] + 3) % 4}
        self.pair = {**at, "xl": 1 - at["xl"]}

    def rows(self, y, xl, piece):
        rows = Q // PIECES
        return self.target.at[pl.ds(pl.multiple_of((y * 2 + xl) * Q + piece * rows, rows), rows)]

    def make(self, kind, piece, source, target, peer):
        sends = Sends(*self.sems)
        sends.used = kind * PIECES + piece
        return sends.make(source, target, peer)

    def pair_copy(self, i):
        at = self.at
        return self.make(0, i, self.source.at[1 - at["xl"], pieces()[i]], self.rows(at["y"], at["xl"], i), self.pair)

    def own_copy(self, i, down):
        at = self.at
        source, target = self.source.at[at["xl"], pieces()[i]], self.rows(at["y"], at["xl"], i)
        return self.make(1 + down, i, source, target, self.down if down else self.up)

    def pair_on(self, i, down):
        got = self.rows(self.at["y"], 1 - self.at["xl"], i)
        return self.make(3 + down, i, got, got, self.down if down else self.up)

    def pass_on(self, i, down):
        at = self.at
        if down:
            got = self.rows((at["y"] + 1) % 4, 1 - at["xl"], i)
        else:
            got = self.rows((at["y"] + 3) % 4, at["xl"], i)
        return self.make(5 + down, i, got, got, self.down if down else self.up)

    def local(self):
        at = self.at
        target = self.target.at[pl.ds(pl.multiple_of((at["y"] * 2 + at["xl"]) * Q, Q), Q)]
        return pltpu.make_async_copy(self.source.at[at["xl"]], target, self.local_sem)

    def begin(self, which=range(PIECES)):
        for i in which:
            self.pair_copy(i).start()
            start_all([self.own_copy(i, down) for down in range(2)])

    def second(self, which=range(PIECES)):
        for i in which:
            self.pair_copy(i).wait()
            start_all([self.pair_on(i, down) for down in range(2)])

    def pass_low(self):
        for i in range(PIECES):
            self.own_copy(i, 0).wait()
            self.pass_on(i, 0).start()

    def third(self):
        self.local().wait()
        for i in range(PIECES):
            self.pair_on(i, 1).wait()
            self.pass_on(i, 1).start()
        for i in range(PIECES):
            self.own_copy(i, 1).wait()
            self.pair_on(i, 0).wait()

    def finish(self):
        wait_all([self.pass_on(i, down) for i in range(PIECES) for down in range(2)])


class RingScatter:
    SEMS = 7 * PIECES

    @staticmethod
    def scratch(width):
        return [pltpu.VMEM((8, Q, width), BF16), dma(RingScatter.SEMS), dma(RingScatter.SEMS)]

    def __init__(self, at, part, refs):
        self.at, self.part = at, part
        self.held, self.ss, self.rs = refs
        y = at["y"]
        self.up_y, self.down_y, self.far_y = (y + 1) % 4, (y + 3) % 4, (y + 2) % 4
        self.up, self.down = {**at, "y": self.up_y}, {**at, "y": self.down_y}
        self.pair = {**at, "xl": 1 - at["xl"]}

    def copy(self, number, i):
        sends = Sends(self.ss, self.rs)
        sends.used = number * PIECES + i
        piece = pieces()[i]
        if number == 6:
            return sends.make(self.held.at[6, piece], self.held.at[7, piece], self.pair)
        y, x = [(self.far_y, 0), (self.far_y, 1), (self.up_y, 1), (self.down_y, 0), (self.up_y, 0), (self.down_y, 1)][number]
        peer = self.down if number % 2 else self.up
        return sends.make(self.part.at[y * 2 + x, piece], self.held.at[number, piece], peer)

    def send_far(self):
        start_all([self.copy(n, i) for i in range(PIECES) for n in range(2)])

    def send_up(self):
        start_all([self.copy(2, i) for i in range(PIECES)])

    def send_down(self):
        start_all([self.copy(3, i) for i in range(PIECES)])

    def second(self):
        for i, piece in enumerate(pieces()):
            for slot, number in ((self.up_y * 2, 0), (self.down_y * 2 + 1, 1)):
                self.copy(number, i).wait()
                total = self.part[slot, piece].astype(F32) + self.held[number, piece].astype(F32)
                self.part[slot, piece] = total.astype(BF16)
                self.copy(4 + number, i).start()

    def third(self, out):
        held, xl, y = self.held, self.at["xl"], self.at["y"]
        for i, piece in enumerate(pieces()):
            wait_all([self.copy(n, i) for n in range(2, 6)])
            totals = []
            for x in range(2):
                total = self.part[y * 2 + x, piece].astype(F32) + held[3 - x, piece].astype(F32)
                totals.append(total + held[4 + x, piece].astype(F32))
            out[xl, piece] = jnp.where(xl == 0, totals[0], totals[1]).astype(BF16)
            held[6, piece] = jnp.where(xl == 0, totals[1], totals[0]).astype(BF16)
            self.copy(6, i).start()

    def finish(self, out):
        wait_all([self.copy(6, i) for i in range(PIECES)])
        out[1 - self.at["xl"]] = self.held[7]


def ring_greets(at):
    return [{**at, "y": (at["y"] + 1) % 4}, {**at, "y": (at["y"] + 3) % 4}, {**at, "xl": 1 - at["xl"]}]


class PlaneGather:
    SEMS = 31

    def __init__(self, at, source, target, send_sems, recv_sems, local_sem, start=0, count=None):
        self.at, self.source, self.target = at, source, target
        self.sems, self.local_sem = (send_sems, recv_sems), local_sem
        depth, part = source.shape[1], source.shape[2]
        self.whole = count is None
        self.start, self.count = start, part if self.whole else count
        self.part = part
        self.upper, self.lower = pl.ds(0, depth // 2), pl.ds(depth // 2, depth // 2)
        self.lanes = pl.ds(self.start, self.count)
        self.cols = pl.ds(pl.multiple_of(at["xl"] * part + self.start, 128), self.count)
        self.both = [pl.ds(0, 2 * part)] if self.whole else [pl.ds(n * part + start, count) for n in range(2)]

    def copies(self, stage):
        at, w = self.at, self.target
        xh, z, c = at["xh"], at["z"], at["c"]
        sends = Sends(*self.sems)
        if stage == 0:
            return [
                sends.make(self.source.at[:, self.upper, self.lanes], w.at[:, xh, z, c, self.upper, self.cols], p)
                for p in x_peers(at)
            ] + [
                sends.make(self.source.at[:, self.lower, self.lanes], w.at[:, xh, z, c, self.lower, self.cols], p)
                for p in z_peers(at)
            ]
        if stage == 1:
            sends.used = 6
            copies = []
            for p in z_peers(at):
                for cols in self.both:
                    up = w.at[:, :, z, c, self.upper, cols]
                    copies.append(sends.make(up, up, p))
            low = w.at[:, xh, :, c, self.lower, self.cols]
            return copies + [sends.make(low, low, p) for p in x_peers(at)]
        sends.used = 15
        copies = []
        for cols in self.both:
            if self.count == 128:
                slots = [w.at[:, :, :, c, :, cols]]
            else:
                slots = [w.at[:, a, b, c, :, cols] for a in range(2) for b in range(4)]
            copies += [sends.make(slot, slot, core_peers(at)[0]) for slot in slots]
        return copies

    def local(self):
        at = self.at
        return pltpu.make_async_copy(
            self.source.at[:, :, self.lanes],
            self.target.at[:, at["xh"], at["z"], at["c"], :, self.cols],
            self.local_sem,
        )

    def begin(self):
        start_all(self.copies(0))
        self.local().start()

    def second(self):
        self.local().wait()
        wait_all(self.copies(0))
        start_all(self.copies(1))

    def third(self):
        wait_all(self.copies(1))
        start_all(self.copies(2))

    def finish(self):
        wait_all(self.copies(2))


class Layout:
    def __init__(self, width):
        self.width, self.half = width, width // 2
        self.part = self.half + 256
        self.total = 2 * self.part
        self.dt_at, self.bc_at = self.half, self.half + 128

    def x(self, v):
        return jnp.concatenate([v[:, : self.half], v[:, self.part : self.part + self.half]], 1)

    def bc(self, v):
        a, b = self.bc_at, self.part + self.bc_at
        return jnp.concatenate([v[:, a : a + 128], v[:, b : b + 128]], 1)

    def dt(self, v, own_heads):
        a, b = self.dt_at, self.part + self.dt_at
        return v[:, a : a + 128] + pltpu.roll(v[:, b : b + 128], own_heads, 1)

    def join(self, x, bc, dt, own_heads):
        lane = lax.broadcasted_iota(jnp.int32, dt.shape, 1)
        first = jnp.where(lane < own_heads, dt, 0.0)
        second = jnp.where(lane < own_heads, pltpu.roll(dt, 128 - own_heads, 1), 0.0)
        return jnp.concatenate(
            [x[:, : self.half], first, bc[:, :128], x[:, self.half :], second, bc[:, 128:]], 1
        )


def own_heads_of(width):
    return width // 128


def chunk_rows(j):
    return pl.ds(pl.multiple_of(j * Q, Q), Q)


def forward_kernel(
    hid, cot_ref, w2_ref,
    ids_ref, wx_ref, wdt_ref, wbc_ref, gain_ref, kx_ref, kxb_ref, kbc_ref, kbcb_ref, og_ref, al_ref, ds_ref, db_ref,
    zx_ref, xin_ref, bcin_ref, dt_ref, bcc_ref, y_ref, start_ref, gon_ref,
    normed_ref, cot_all_ref, w2_all_ref, wxe_all_ref, stat_ref, small_all, tok_all,
    wxe, bc_got, bc_rows, held, lanes,
    pick_ref, state, xh, bch, hids, wxes, xes, cots, weights, normeds, ys, stats, stat_held,
    hid_send, hid_recv, bc_send, bc_recv, w_send, w_recv, wbc_send, wbc_recv, small_send, small_recv,
    cot_send, cot_recv, w2_send, w2_recv, stat_send, stat_recv, sems,
):
    step = pl.program_id(0)
    steps = (pl.num_programs(0) - 1) // 2
    per_step = STEP_ROWS // Q
    width = zx_ref.shape[2]
    lay = Layout(width)
    pairs = width // 128
    chunks = stats.shape[0] // 2
    own_heads = wdt_ref.shape[0]
    depth, half = wx_ref.shape
    at = place()
    y, xl = at["y"], at["xl"]
    peers = group_peers(at)
    ring = RingGather(at, hid, hids, hid_send, hid_recv, sems.at[0])
    ring_cot = RingGather(at, cot_ref, cots, cot_send, cot_recv, sems.at[1])
    plane = PlaneGather(at, wxe, wxes, w_send, w_recv, sems.at[2], 0, half + 128)
    plane_bc = PlaneGather(at, wxe, wxes, wbc_send, wbc_recv, sems.at[3], half + 128, 128)
    plane_w2 = PlaneGather(at, w2_ref, weights, w2_send, w2_recv, sems.at[4])
    small_ref, tok_ref = small_all, tok_all

    def results():
        pairs_of = [(wxes, wxe_all_ref), (normeds, normed_ref), (cots, cot_all_ref), (weights, w2_all_ref)]
        return [pltpu.make_async_copy(a, b, sems.at[5 + i]) for i, (a, b) in enumerate(pairs_of)]

    @pl.when(step == 0)
    def _():
        greets = peers + plane_greets(at) + y_core_peers(at)[4:]
        greet_begin(greets)
        bc_slot = bc_got.at[y * 2 + xl]
        wxe[0, :, 0:half] = wx_ref[...]
        lanes[...] = jnp.zeros_like(lanes)
        lanes[0:own_heads, 0:depth] = wdt_ref[...].astype(F32)
        wxe[0, :, half : half + 128] = columns_of(lanes[:, 0:128])[0:depth].astype(BF16)
        lanes[...] = jnp.zeros_like(lanes)
        lanes[0:2, 0:4] = kbc_ref[...].astype(F32)
        taps_bc = columns_of(lanes[:, 0:128])[0:4, 0:2]
        bc_got[y * 2 + xl, 0:12] = wbc_ref[...].astype(F32)

        def placed(pieces, width, start):
            lanes[...] = jnp.zeros_like(lanes)
            row = 0
            for piece in pieces:
                count, size = piece.shape
                lanes[row : row + count, 0:size] = piece[...].astype(F32)
                row += count
            return pltpu.roll(lanes[:, 0:width], start, 1)

        dp = at["xh"] * 8 + at["z"] * 2 + at["c"]
        everyone = dp * 8 + y * 2 + xl
        small_all[...] = jnp.zeros_like(small_all)
        value = placed([taps_bc, kbcb_ref], 256, everyone * kbc_ref.shape[0])
        for t in range(5):
            put_wide(small_all, BC_TAPS + 2 * t, value[t : t + 1])
        value = placed([gain_ref], lanes.shape[1], everyone * gain_ref.shape[1])
        put_wide(small_all, IN_GAIN, value[0:1])
        value = placed([kx_ref, kxb_ref, og_ref], 2 * half, xl * half + dp * kx_ref.shape[1])
        for t in range(6):
            put_wide(small_all, X_TAPS + t * (half // 64), value[t : t + 1])
        value = placed([al_ref, ds_ref, db_ref], 128, xl * own_heads)
        small_all[HEAD_ROWS : HEAD_ROWS + 3] = jnp.where(dp == 0, value[0:3], 0.0)
        greet_end(greets)
        sends = Sends(bc_send, bc_recv)
        bc_copies = [sends.start(bc_slot, bc_slot, p) for p in peers]
        small_sends = Sends(small_send, small_recv)
        small = YCoreExchange(at, small_all, held, small_sends)
        ring.local().start()
        ring_cot.local().start()
        ring.begin(range(0, 1))
        plane.begin()
        ids = ids_ref[pl.ds(xl, 1), :]
        token_info(jnp.concatenate([ids[:, n * Q : n * Q + Q] for n in range(chunks)], 0), tok_all)
        pick_ref[...] = head_pick(width)
        state[...] = jnp.zeros_like(state)
        xh[0:HALO] = jnp.zeros((HALO, width), F32)
        bch[0:HALO] = jnp.zeros((HALO, bch.shape[1]), F32)

        wait_all(bc_copies)
        for m in range(8):
            bc_rows[12 * m : 12 * m + 12] = bc_got[m, 0:12]
        wxe[0, :, half + 128 : half + 256] = half_of(bc_rows[...], xl).astype(BF16)
        small.finish()
        small = Exchange(small_all, SMALL_ROWS, x_peers(at), held.at[7:10], small_sends)
        plane_bc.begin()
        ring.begin(range(1, 2))
        ring.second(range(0, 1))
        small.finish()
        small = Exchange(small_all, SMALL_ROWS, z_peers(at), held.at[10:13], small_sends)
        plane.second()
        plane_bc.second()
        ring.second(range(1, 2))
        ring.pass_low()
        small.finish()
        ring.third()
        ring_cot.begin()
        plane.third()
        plane_bc.third()
        plane_w2.begin()
        plane.finish()
        plane_bc.finish()

        def project(number):
            rows = block_rows((y + number) % 4)
            value = hids[rows].astype(F32)
            inv_rms = lax.rsqrt(jnp.mean(value * value, -1, keepdims=True) + EPS)
            normed = (value * inv_rms * wide(small_ref, IN_GAIN, 12)).astype(BF16)
            normeds[rows] = normed
            xes[rows] = dot(normed, wxes[0].reshape(hids.shape[1], lay.total))

        @pl.loop(0, 3)
        def _(n):
            project(n + n // 2)

        ring_cot.second()
        plane_w2.second()
        ring.finish()
        project(2)
        ring_cot.pass_low()
        start_all(results()[:2])

    @pl.when(step == 3)
    def _():
        ring_cot.third()

    @pl.when((step >= 1) & (step <= steps))
    def _():
        @pl.loop(0, per_step)
        def _(j):
            chunk = (step - 1) * per_step + j
            here = chunk_rows(j)

            @pl.when(chunk > 0)
            def _():
                xh[0:HALO] = xh[Q : Q + HALO]
                bch[0:HALO] = bch[Q : Q + HALO]

            @pl.when(chunk == 5)
            def _():
                plane_w2.third()

            rows16 = tok_ref[chunk]
            tok = columns_of(rows16)
            hp = small_ref[HEAD_ROWS : HEAD_ROWS + 3]
            pick = pick_ref[...]
            xe = xes[chunk_rows(chunk)]
            x_in, bc_in, dt_in = lay.x(xe), lay.bc(xe), lay.dt(xe, own_heads)
            xin_ref[here] = x_in.astype(BF16)
            bcin_ref[here] = bc_in.astype(BF16)
            dt_ref[here] = dt_in

            def conv(held_rows, new, row, count):
                held_rows[HALO : HALO + Q] = new
                taps = [wide(small_ref, row + t * count, count) for t in range(5)]
                out = taps[4] + taps[3] * new
                for t in range(1, 4):
                    out = out + (taps[3 - t] * held_rows[HALO - t : HALO - t + Q]) * lanes_of(tok, KEEP + t)
                return out

            xc = conv(xh, x_in, X_TAPS, pairs)
            bcc = conv(bch, bc_in, BC_TAPS, 2)
            zx_ref[0, here] = xc
            bcc_ref[here] = bcc
            x_act = xc * sigmoid(xc)
            bc_act = bcc * sigmoid(bcc)
            n = bc_act.shape[1] // 2
            b_low = bc_act[:, :n].astype(BF16)
            c_low = bc_act[:, n:].astype(BF16)
            size, rate, cum2, cum2_t, enter, leave, keep = decays(dt_in, hp, tok)
            same = causal() & (lanes_of(tok, SEG) == rows16[SEG : SEG + 1])
            scores = jnp.where(same, dot(c_low, b_low, NT), 0.0)
            xs = x_act * expand(size, pick)
            xs_low = xs.astype(BF16)
            before = state[...]
            before_low = before.astype(BF16)
            start_ref[j] = before_low
            inter = dot(c_low, before_low) * expand(enter, pick)
            outs = []
            for pair in range(pairs):
                mixes = [(scores * gaps(cum2, cum2_t, 2 * pair + i)).astype(BF16) for i in range(2)]
                outs.append(
                    dot(jnp.concatenate(mixes, 1), pair_blocks(xs_low[:, pair * 128 : pair * 128 + 128]))
                )
            skip = expand(jnp.broadcast_to(hp[1:2], (8, 128)), pick)[0:1]
            y = jnp.concatenate(outs, 1) + inter + skip * x_act
            y_ref[here] = y
            ys[chunk_rows(chunk)] = y
            moved = (xs * expand(leave, pick)).astype(BF16)
            keep_all = expand(jnp.broadcast_to(keep, (8, 128)), pick)[0:1]
            state[...] = before * keep_all + dot(b_low, moved, TN)

    full = hids.shape[1]

    @pl.when(step == steps + 1)
    def _():
        plane_w2.finish()

        @pl.loop(0, steps)
        def _(number):
            rows = block_rows(number)
            z = dot(normeds[rows], weights[0].reshape(full, width))
            xes[rows, 0:width] = z
            gated = ys[rows] * (z * sigmoid(z))
            ys[rows] = gated
            for j in range(per_step):
                value = gated[j * Q : j * Q + Q]
                stats[pl.ds(number * per_step + j, 1), :] = row_sums(value * value)

        results()[3].start()

    @pl.when(step == 2 * steps)
    def _():
        ring_cot.finish()
        results()[2].start()

    @pl.when(step > steps)
    def _():
        number = arrival_block(step - steps - 1, y)
        rows = block_rows(number)
        zx_ref[0] = xes[rows, 0:width]
        gon = dot(cots[rows], weights[1].reshape(full, width))
        gon_ref[...] = gon.astype(BF16)
        inner = ys[rows] * (gon * wide(small_ref, X_TAPS + 5 * pairs, pairs))
        for j in range(per_step):
            stats[pl.ds(chunks + number * per_step + j, 1), :] = row_sums(inner[j * Q : j * Q + Q])

    @pl.when(step == 2 * steps)
    def _():
        sums = Exchange(stats, stats.shape[0], y_peers(at), stat_held, Sends(stat_send, stat_recv))
        wait_all(results())
        sums.finish()
        inner = width * 4
        scale = lax.rsqrt(stats[0:chunks] / inner + EPS)
        stat_ref[0:chunks] = scale
        stat_ref[chunks : 2 * chunks] = scale * scale * scale * stats[chunks : 2 * chunks] / inner


def row_sums(values):
    total = values[:, 0:128]
    for start in range(128, values.shape[1], 128):
        total = total + values[:, start : start + 128]
    return jnp.sum(total.T, axis=0, keepdims=True)


def half_of(value, xl):
    half = value.shape[-1] // 2
    return jnp.where(xl == 0, value[..., :half], value[..., half:])


class PlaneSum:
    SEMS = 20

    @staticmethod
    def scratch(depth, width):
        cut, half = depth // 2, width // 2
        return [
            pltpu.VMEM((2, 4, depth, width), BF16),
            pltpu.VMEM((3, 4, cut, half), BF16),
            pltpu.VMEM((3, 2, cut, width), BF16),
            pltpu.VMEM((4, cut, half), BF16),
            pltpu.VMEM((2, cut, width), BF16),
            pltpu.VMEM((3, cut, half), BF16),
            pltpu.VMEM((3, cut, half), BF16),
            dma(PlaneSum.SEMS),
            dma(PlaneSum.SEMS),
        ]

    def __init__(self, at, source, refs):
        self.at, self.source = at, source
        (self.got, self.a2, self.b2, self.sa, self.sb, self.a3, self.b3, self.ss, self.rs) = refs
        self.depth, self.width = self.got.shape[2], self.got.shape[3]
        self.cut, self.half = self.depth // 2, self.width // 2

    def columns(self, xl):
        return pl.ds(pl.multiple_of(xl * self.half, 128), self.half)

    def sends(self, used):
        sends = Sends(self.ss, self.rs)
        sends.used = used
        return sends

    def first(self, xh, z):
        peer = core_peers(self.at)[0]
        source = self.source.at[xh, z, peer["c"], :, pl.ds(0, self.width)]
        return self.sends(xh * 4 + z).make(source, self.got.at[xh, z], peer)

    def second_x(self, number):
        p, c = x_peers(self.at)[number], self.at["c"]
        source = self.source.at[p["xh"], :, c, pl.ds(0, self.cut), self.columns(p["xl"])]
        return self.sends(8 + number).make(source, self.a2.at[number], p)

    def second_z(self, number):
        p, c = z_peers(self.at)[number], self.at["c"]
        source = self.source.at[:, p["z"], c, pl.ds(self.cut, self.cut), pl.ds(0, self.width)]
        return self.sends(11 + number).make(source, self.b2.at[number], p)

    def third(self):
        sends = self.sends(14)
        copies = []
        for i, p in enumerate(z_peers(self.at)):
            copies.append(sends.make(self.sa.at[p["z"]], self.a3.at[i], p))
        for i, p in enumerate(x_peers(self.at)):
            copies.append(sends.make(self.sb.at[p["xh"], :, self.columns(p["xl"])], self.b3.at[i], p))
        return copies

    def after_cores(self):
        c = self.at["c"]
        for far in (1, 0):
            xh = (self.at["xh"] + far) % 2
            for z in range(4):
                self.first(xh, z).wait()
                total = self.source[xh, z, c, :, 0 : self.width].astype(F32) + self.got[xh, z].astype(F32)
                self.source[xh, z, c, :, 0 : self.width] = total.astype(BF16)
            start_all([self.second_x(n) for n in ((1, 2) if far else (0,))])
        start_all([self.second_z(n) for n in range(3)])

    def after_first_axis(self):
        wait_all([self.second_x(n) for n in range(3)] + [self.second_z(n) for n in range(3)])
        at, cut, width = self.at, self.cut, self.width
        c = at["c"]

        @pl.loop(0, 4)
        def _(z):
            total = half_of(self.source[at["xh"], z, c, 0:cut, 0:width], at["xl"]).astype(F32)
            for i in range(3):
                total = total + self.a2[i, z].astype(F32)
            self.sa[z] = total.astype(BF16)

        for xh in range(2):
            total = self.source[xh, at["z"], c, cut : 2 * cut, 0:width].astype(F32)
            for i in range(3):
                total = total + self.b2[i, xh].astype(F32)
            self.sb[xh] = total.astype(BF16)
        start_all(self.third())

    def finish(self, out):
        wait_all(self.third())
        at, cut = self.at, self.cut
        total = self.sa[at["z"]].astype(F32)
        for i in range(3):
            total = total + self.a3[i].astype(F32)
        out[0:cut] = total
        total = half_of(self.sb[at["xh"]], at["xl"]).astype(F32)
        for i in range(3):
            total = total + self.b3[i].astype(F32)
        out[cut : 2 * cut] = total


def plane_greets(at):
    return x_peers(at)[1:] + z_peers(at) + core_peers(at)


PRE, MIX = 4, 4


def arrival_block(step, y):
    return (y + step + jnp.where(step == 2, 1, jnp.where(step == 3, 3, 0))) % 4


def owner_block(step, y):
    return (y + jnp.where(step == 0, 2, jnp.where(step == 1, 1, jnp.where(step == 2, 3, 0)))) % 4


def block_rows(number):
    return pl.ds(pl.multiple_of(number * STEP_ROWS, STEP_ROWS), STEP_ROWS)


def backward_kernel(
    tok_ref, stat_ref, small_ref, zx_ref, gon_ref, y_ref, xin_ref, bcin_ref, dt_ref, bcc_ref, start_ref,
    cot_ref, normed_ref, w2_ref, wxe_ref,
    out_ref, back_ref, gzo_ref, gxe_ref, sums_ref, bcs_ref,
    pick_ref, adjoint, dh, dbh, gkx, gkbc, ghead, cots, normeds, weight, wxe, outs_low, z_low, dy_all, part, source,
    held, bc_got, small_send, small_recv, bc_send, bc_recv, sems, *refs,
):
    step = pl.program_id(0)
    per_step = STEP_ROWS // Q
    width = zx_ref.shape[2]
    pairs = width // 128
    own_heads = own_heads_of(width)
    lay = Layout(width)
    chunks = tok_ref.shape[0]
    model = cots.shape[1]
    depth = model // 16
    at = place()
    ring_out = RingScatter(at, part, refs[0:3])
    ring_in = RingScatter(at, part, refs[3:6])
    plane_zo = PlaneSum(at, source, refs[6:15])
    plane_xe = PlaneSum(at, source, refs[15:24])
    peers = group_peers(at)
    loads = [
        pltpu.make_async_copy(a, b, sems.at[n])
        for n, (a, b) in enumerate(
            [(w2_ref.at[1], weight), (cot_ref, cots), (normed_ref, normeds), (wxe_ref, wxe), (w2_ref.at[0], weight)]
        )
    ]

    def put_part(owner, value):
        low = value.astype(BF16)
        for x in range(2):
            part[owner * 2 + x] = low[x * Q : x * Q + Q]

    def put_grads(plane, terms):
        for quarter in range(4):
            cut = slice(quarter * (model // 4), (quarter + 1) * (model // 4))
            xh, z = quarter // 2, (quarter % 2) * 2
            for left, right, start, part in terms:
                value = dot(left[:, cut], right, TN).astype(BF16)
                half = value.shape[1] // 2
                value = value.reshape(2, 2, model // 16, 2 * half)
                for n in range(2):
                    first = n * part + start
                    source[xh, z : z + 2, :, :, first : first + half] = value[..., n * half : n * half + half]
            start_all([plane.first(xh, z), plane.first(xh, z + 1)])

    @pl.when(step == 0)
    def _():
        start_all(loads[:4])
        greet_begin(peers + plane_greets(at) + y_core_peers(at)[4:])
        pick_ref[...] = head_pick(width)
        adjoint[...] = jnp.zeros_like(adjoint)
        dh[...] = jnp.zeros_like(dh)
        dbh[...] = jnp.zeros_like(dbh)
        gkx[...] = jnp.zeros_like(gkx)
        gkbc[...] = jnp.zeros_like(gkbc)
        ghead[...] = jnp.zeros_like(ghead)
        loads[0].wait()

    @pl.when(step < PRE)
    def _():
        owner = owner_block(step, at["y"])
        rows = block_rows(owner)
        columns = []
        for j in range(per_step):
            chunk = owner * per_step + j
            columns.append(
                columns_of(jnp.concatenate([stat_ref[pl.ds(chunk, 1), :], stat_ref[pl.ds(chunks + chunk, 1), :]], 0))
            )
        columns = jnp.concatenate(columns, 0)
        scale, coef = columns[:, 0:1], columns[:, 1:2]
        gain = wide(small_ref, X_TAPS + 5 * pairs, pairs)
        z, y, gon = zx_ref[0], y_ref[...], gon_ref[...].astype(F32)
        z_sig = sigmoid(z)
        z_act = z * z_sig
        gated = y * z_act
        scaled = gated * scale
        out_low = (scaled * gain).astype(BF16)
        outs_low[rows] = out_low
        gkx[5] += rows8(gon * scaled)
        grad_gated = scale * (gon * gain) - gated * coef
        dy_all[rows] = (grad_gated * z_act).astype(BF16)
        z_low[rows] = (grad_gated * y * (z_sig * (1.0 + z * (1.0 - z_sig)))).astype(BF16)
        put_part(owner, dot(out_low, weight[...], NT))

    @pl.when(step == 0)
    def _():
        greet_end(peers + plane_greets(at) + y_core_peers(at)[4:])
        ring_out.send_far()

    @pl.when(step == 1)
    def _():
        ring_out.send_up()

    @pl.when(step == 2)
    def _():
        ring_out.send_down()

    @pl.when(step == PRE)
    def _():
        loads[4].start()
        loads[1].wait()
        loads[2].wait()
        put_grads(
            plane_zo, [(cots, outs_low[...], width // 2, width), (normeds, z_low[...], 0, width)]
        )
        ring_out.second()

    @pl.when(step == PRE + 1)
    def _():
        plane_zo.after_cores()

    @pl.when(step == PRE + 3)
    def _():
        ring_out.third(out_ref)

    @pl.when((step >= PRE) & (step < PRE + MIX))
    def _():
        @pl.loop(0, per_step)
        def _(turn_in):
            j = per_step - 1 - turn_in
            chunk = (PRE + MIX - 1 - step) * per_step + j
            here = chunk_rows(j)
            there = chunk_rows(chunk)

            @pl.when(chunk < chunks - 1)
            def _():
                dh[Q : Q + HALO] = dh[0:HALO]
                dbh[Q : Q + HALO] = dbh[0:HALO]

            @pl.when(chunk == 0)
            def _():
                plane_zo.after_first_axis()

            rows16 = tok_ref[chunk]
            tok = columns_of(rows16)
            hp = small_ref[HEAD_ROWS : HEAD_ROWS + 3]
            pick = pick_ref[...]
            dt_in = dt_ref[here]
            xc = zx_ref[0, here]
            bcc = bcc_ref[here]
            x_sig = sigmoid(xc)
            x_act = xc * x_sig
            bc_sig = sigmoid(bcc)
            bc_act = bcc * bc_sig
            n = bc_act.shape[1] // 2
            b_low = bc_act[:, :n].astype(BF16)
            c_low = bc_act[:, n:].astype(BF16)
            size, rate, cum2, cum2_t, enter, leave, keep = decays(dt_in, hp, tok)
            same = causal() & (lanes_of(tok, SEG) == rows16[SEG : SEG + 1])
            scores = jnp.where(same, dot(c_low, b_low, NT), 0.0)
            step_all = expand(size, pick)
            leave_all = expand(leave, pick)
            xs = x_act * step_all
            xs_low = xs.astype(BF16)
            moved = (xs * leave_all).astype(BF16)
            dy_low = dy_all[there]
            dy = dy_low.astype(F32)
            dy_in = (dy * expand(enter, pick)).astype(BF16)

            skip = expand(jnp.broadcast_to(hp[1:2], (8, 128)), pick)[0:1]
            before_low = start_ref[j]
            after = adjoint[...]
            after_low = after.astype(BF16)

            from_state = dot(b_low, after_low)
            outs = []
            dscores = jnp.zeros((Q, Q), F32)
            for pair in range(pairs):
                cut = slice(pair * 128, pair * 128 + 128)
                dys = pair_blocks(dy_low[:, cut])
                inner = dot(dys, xs_low[:, cut], NT)
                mixes = []
                for i in range(2):
                    gap = gaps(cum2, cum2_t, 2 * pair + i)
                    mixes.append((scores * gap).astype(BF16))
                    dscores = dscores + inner[i * Q : i * Q + Q] * gap
                outs.append(dot(jnp.concatenate(mixes, 0), dys, TN))
            intra = jnp.concatenate(outs, 1)
            dscores = jnp.where(same, dscores, 0.0).astype(BF16)

            dxs = intra + leave_all * from_state
            dx_act = dxs * step_all + skip * dy
            gkx[6] += rows8(dy * x_act)
            plus = head_sums(dy * (y_ref[here] - skip * x_act), pick)
            through = moved.astype(F32) * from_state
            minus = head_sums(xs_low.astype(F32) * intra + through, pick)
            direct = head_sums(dxs * x_act, pick)
            keep_all = expand(jnp.broadcast_to(keep, (8, 128)), pick)[0:1]
            at_end = rows8(through) + keep_all * rows8(after * before_low.astype(F32))
            at_end = jnp.sum(head_sums(at_end, pick), axis=0, keepdims=True)
            last_row = lax.broadcasted_iota(jnp.int32, (Q, 128), 0) == Q - 1
            dcum = plus - minus + jnp.where(last_row, at_end, 0.0)
            tri = jnp.where(causal(), 1.0, 0.0)
            drate = dot_exact(tri, dcum, TN)
            dstep = direct - jnp.exp(hp[0:1]) * drate
            ddt = dstep * sigmoid(dt_in + hp[2:3])
            ghead[0] += rows8(drate * rate)
            ghead[1] += rows8(ddt)

            dc = dot(dscores, b_low) + dot(dy_in, before_low, NT)
            db = dot(dscores, c_low, TN) + dot(moved, after_low, NT)
            adjoint[...] = keep_all * after + dot(c_low, dy_in, TN)

            def conv_back(held_rows, grad, new, row, count, out):
                held_rows[0:Q] = grad
                taps = [wide(small_ref, row + t * count, count) for t in range(4)]
                total = taps[3] * grad
                out[3] += rows8(new * grad)
                out[4] += rows8(grad)
                for t in range(1, 4):
                    piece = held_rows[t : t + Q] * lanes_of(tok, AHEAD + t)
                    total = total + taps[3 - t] * piece
                    out[3 - t] += rows8(new * piece)
                return total

            dxc = dx_act * (x_sig * (1.0 + xc * (1.0 - x_sig)))
            dx_in = conv_back(dh, dxc, xin_ref[here].astype(F32), X_TAPS, pairs, gkx)
            dbcc = jnp.concatenate([db, dc], 1) * (bc_sig * (1.0 + bcc * (1.0 - bc_sig)))
            dbc_in = conv_back(dbh, dbcc, bcin_ref[here].astype(F32), BC_TAPS, 2, gkbc)
            cots[there, 0 : lay.total] = lay.join(dx_in, dbc_in, ddt, own_heads).astype(BF16)

    @pl.when(step == PRE + MIX)
    def _():
        sums_ref[...] = jnp.zeros_like(sums_ref)
        for t in range(5):
            put_wide(sums_ref, 2 * t, jnp.sum(gkbc[t], axis=0, keepdims=True))
        for t in range(7):
            put_wide(sums_ref, X_TAPS + t * pairs, jnp.sum(gkx[t], axis=0, keepdims=True))
        for t in range(2):
            put_wide(sums_ref, X_TAPS + 7 * pairs + t, jnp.sum(ghead[t], axis=0, keepdims=True))
        small_sends = Sends(small_send, small_recv)
        small = YCoreExchange(at, sums_ref, held, small_sends)
        loads[3].wait()
        loads[4].wait()

        def part_in(number):
            owner = (at["y"] + number) % 4
            rows = block_rows(owner)
            put_part(owner, dot(z_low[rows], weight[...], NT) + dot(cots[rows, 0 : lay.total], wxe[...], NT))

        put_grads(plane_xe, [(normeds, cots[:, 0 : lay.total], 0, lay.part)])
        small.finish()
        small = Exchange(sums_ref, sums_ref.shape[0], x_peers(at), held.at[7:10], small_sends)
        part_in(2)
        ring_in.send_far()
        small.finish()
        small = Exchange(sums_ref, sums_ref.shape[0], z_peers(at), held.at[10:13], small_sends)
        plane_xe.after_cores()
        part_in(1)
        ring_in.send_up()
        part_in(3)
        ring_in.send_down()
        part_in(0)
        ring_in.second()
        small.finish()
        ring_out.finish(out_ref)
        plane_zo.finish(gzo_ref)
        plane_xe.after_first_axis()
        ring_in.third(back_ref)
        plane_xe.finish(gxe_ref)

        dp = at["xh"] * 8 + at["z"] * 2 + at["c"]
        own = pl.ds(pl.multiple_of(dp * depth, 16), depth)
        terms = half_of(weight[own], at["xl"]).astype(F32) * gzo_ref[:, 0 : lay.half]
        total = terms[:, 0:128] + terms[:, 128:256] + terms[:, 256:384]
        terms = half_of(wxe[own], at["xl"]).astype(F32) * gxe_ref[...]
        for n in range(lay.part // 128):
            total = total + terms[:, n * 128 : n * 128 + 128]
        total = jnp.concatenate([total, jnp.zeros((128 - depth, 128), F32)], 0)
        bc_got[at["xl"], at["y"], 0:depth] = gxe_ref[:, lay.bc_at : lay.bc_at + 128]
        bc_got[at["xl"], at["y"], depth : depth + 8] = jnp.broadcast_to(jnp.sum(total.T, axis=0, keepdims=True), (8, 128))
        slot = bc_got.at[at["xl"], at["y"]]
        sends = Sends(bc_send, bc_recv)
        bc_copies = [sends.start(slot, slot, p) for p in peers]
        ring_in.finish(back_ref)
        wait_all(bc_copies)
        for n in range(2):
            bcs_ref[n] = jnp.sum(bc_got[n], axis=0)


def put_wide(ref, row, value):
    for i in range(value.shape[1] // 128):
        ref[row + i : row + i + 1] = value[:, i * 128 : i * 128 + 128]


def block(rows, w, index):
    return pl.BlockSpec((rows, w), lambda i: (index(i), 0))


def whole(shape):
    return pl.BlockSpec(shape, lambda i: (0,) * len(shape), pipeline_mode=pl.Buffered(1))


def whole_out(shape):
    return pl.BlockSpec(shape, lambda i: (0,) * len(shape))


ANY = pl.BlockSpec(memory_space=pl.ANY)
IN_VMEM = pl.BlockSpec(memory_space=pltpu.VMEM)


def like(shape, dtype):
    return jax.ShapeDtypeStruct(shape, dtype)


def dma(count):
    return pltpu.SemaphoreType.DMA((count,))


def remote_params(cid):
    return pltpu.CompilerParams(collective_id=cid, has_side_effects=True, vmem_limit_bytes=VMEM_LIMIT)


def forward_call(hidden, cotangent, w2, ids, w_x, w_dt, w_bc, small_args):
    _, rows, model = hidden.shape
    _, depth, half = w2.shape
    width, part = 2 * half, half + 256
    length = 8 * rows
    steps = length // STEP_ROWS
    chunks = length // Q
    args = [ids, w_x, w_dt, w_bc, *small_args]

    def early(i):
        return jnp.clip(i - 1, 0, steps - 1)

    def late(i):
        return arrival_block(jnp.maximum(i - steps - 1, 0), lax.axis_index("mp") // 2)

    return pl.pallas_call(
        forward_kernel,
        grid=(2 * steps + 1,),
        in_specs=[ANY, ANY, ANY] + [whole(arg.shape) for arg in args],
        out_specs=[pl.BlockSpec((1, STEP_ROWS, width), lambda i: (jnp.where(i > steps, 1, 0), jnp.where(i > steps, late(i), early(i)), 0)),
                   block(STEP_ROWS, width, early), block(STEP_ROWS, 256, early),
                   block(STEP_ROWS, 128, early), block(STEP_ROWS, 256, early), block(STEP_ROWS, width, early),
                   pl.BlockSpec((STEP_ROWS // Q, 128, width), lambda i: (early(i), 0, 0)),
                   block(STEP_ROWS, width, late), ANY, ANY, ANY, ANY,
                   whole_out((2 * chunks, Q)), whole_out((SMALL_ROWS, 128)), whole_out((chunks, 16, Q))],
        out_shape=[
            like((2, length, width), F32), like((length, width), BF16), like((length, 256), BF16),
            like((length, 128), F32),
            like((length, 256), F32), like((length, width), F32), like((chunks, 128, width), BF16),
            like((length, width), BF16), like((length, model), BF16), like((length, model), BF16),
            like((2, 2, 4, 2, depth, width), BF16), like((1, 2, 4, 2, depth, 2 * part), BF16),
            like((2 * chunks, Q), F32), like((SMALL_ROWS, 128), F32), like((chunks, 16, Q), F32),
        ],
        scratch_shapes=[
            pltpu.VMEM((1, depth, part), BF16),
            pltpu.VMEM((8, 16, w_bc.shape[1]), F32),
            pltpu.VMEM((depth, w_bc.shape[1]), F32),
            pltpu.VMEM((13, SMALL_ROWS, 128), F32),
            pltpu.VMEM((8, model), F32),
            pltpu.VMEM((width, 128), BF16),
            pltpu.VMEM((128, width), F32),
            pltpu.VMEM((Q + HALO, width), F32),
            pltpu.VMEM((Q + HALO, 256), F32),
            pltpu.VMEM((length, model), BF16),
            pltpu.VMEM((1, 2, 4, 2, depth, 2 * part), BF16),
            pltpu.VMEM((length, 2 * part), F32),
            pltpu.VMEM((length, model), BF16),
            pltpu.VMEM((2, 2, 4, 2, depth, width), BF16),
            pltpu.VMEM((length, model), BF16),
            pltpu.VMEM((length, width), F32),
            pltpu.VMEM((2 * chunks, Q), F32),
            pltpu.VMEM((3, 2 * chunks, Q), F32),
            dma(RingGather.SEMS), dma(RingGather.SEMS), dma(7), dma(7), dma(31), dma(31), dma(31), dma(31), dma(13), dma(13),
            dma(RingGather.SEMS), dma(RingGather.SEMS), dma(31), dma(31), dma(3), dma(3), dma(9),
        ],
        name="mix_forward",
        compiler_params=remote_params(1),
    )(hidden, cotangent, w2, *args)


def backward_call(tok, stat, small, zx, gon, y, xin, bcin, dt, bcc, starts, cots, normed, w2, wxe):
    length, width = y.shape
    model, total = wxe.shape
    depth = model // 16
    steps = length // STEP_ROWS

    def both(i):
        first = owner_block(i, lax.axis_index("mp") // 2)
        return jnp.where(i < PRE, first, jnp.maximum(PRE + MIX - 1 - i, 0))

    def mix(i):
        return jnp.clip(PRE + MIX - 1 - i, 0, steps - 1)

    def pre(i):
        return owner_block(jnp.minimum(i, PRE - 1), lax.axis_index("mp") // 2)

    return pl.pallas_call(
        backward_kernel,
        grid=(PRE + MIX + 1,),
        in_specs=[whole(tok.shape), whole(stat.shape), whole(small.shape),
                  pl.BlockSpec((1, STEP_ROWS, width), lambda i: (jnp.where(i < PRE, 1, 0), both(i), 0)),
                  block(STEP_ROWS, width, pre), block(STEP_ROWS, width, both),
                  block(STEP_ROWS, width, mix), block(STEP_ROWS, 256, mix), block(STEP_ROWS, 128, mix),
                  block(STEP_ROWS, 256, mix),
                  pl.BlockSpec((STEP_ROWS // Q, 128, width), lambda i: (mix(i), 0, 0)), ANY, ANY, ANY, ANY],
        out_specs=[whole((2, Q, model)), whole((2, Q, model)), whole((depth, width)), whole((depth, total // 2)),
                   whole((72, 128)), whole((2, depth + 8, 128))],
        out_shape=[
            like((2, Q, model), BF16), like((2, Q, model), BF16), like((depth, width), F32),
            like((depth, total // 2), F32), like((72, 128), F32), like((2, depth + 8, 128), F32),
        ],
        scratch_shapes=[
            pltpu.VMEM((width, 128), BF16),
            pltpu.VMEM((128, width), F32),
            pltpu.VMEM((Q + HALO, width), F32),
            pltpu.VMEM((Q + HALO, 256), F32),
            pltpu.VMEM((7, 8, width), F32),
            pltpu.VMEM((5, 8, 256), F32),
            pltpu.VMEM((2, 8, 128), F32),
            pltpu.VMEM((length, model), BF16),
            pltpu.VMEM((length, model), BF16),
            pltpu.VMEM((model, width), BF16),
            pltpu.VMEM((model, total), BF16),
            pltpu.VMEM((length, width), BF16),
            pltpu.VMEM((length, width), BF16),
            pltpu.VMEM((length, width), BF16),
            pltpu.VMEM((8, Q, model), BF16),
            pltpu.VMEM((2, 4, 2, depth, 2 * width), BF16),
            pltpu.VMEM((13, 72, 128), F32),
            pltpu.VMEM((2, 4, depth + 8, 128), F32),
            dma(13), dma(13), dma(7), dma(7), dma(5),
            *RingScatter.scratch(model),
            *RingScatter.scratch(model),
            *PlaneSum.scratch(depth, 2 * width),
            *PlaneSum.scratch(depth, total),
        ],
        name="mix_backward",
        compiler_params=remote_params(2),
    )(tok, stat, small, zx, gon, y, xin, bcin, dt, bcc, starts, cots, normed, w2, wxe)


def token_info(ids, out):
    chunks = ids.shape[0]
    seg = ids.astype(F32)
    lane = lax.broadcasted_iota(jnp.int32, seg.shape, 1)
    row = lax.broadcasted_iota(jnp.int32, seg.shape, 0)

    def chunk_back(v):
        return jnp.where(row == 0, -1.0, pltpu.roll(v, 1, 0))

    def chunk_ahead(v):
        return jnp.where(row == chunks - 1, -1.0, pltpu.roll(v, chunks - 1, 0))

    def flag(mask):
        return jnp.where(mask, 1.0, 0.0)

    tail = jnp.broadcast_to(seg[:, Q - 1 :], seg.shape)
    last = chunk_back(tail)
    rows = {SEG: seg, ENTER: flag(seg == last), LEAVE: flag(seg == tail), CARRY: flag(tail == last)}
    for j in range(1, 4):
        turned = pltpu.roll(seg, j, 1)
        rows[KEEP + j] = flag(jnp.where(lane < j, chunk_back(turned), turned) == seg)
        turned = pltpu.roll(seg, Q - j, 1)
        rows[AHEAD + j] = flag(jnp.where(lane >= Q - j, chunk_ahead(turned), turned) == seg)
    out[...] = jnp.zeros_like(out)
    for number, value in rows.items():
        for chunk in range(chunks):
            out[chunk, number : number + 1] = value[chunk : chunk + 1]


def finish_kernel(
    hid, cot, got, back, small, gain, gzo, gxe, sums, bcs,
    mixed, g_hid, g_gain, g_wz, g_wx, g_wdt, g_wbc, g_kx, g_kxb, g_kbc, g_kbcb, g_al, g_ds, g_db, g_og, g_wo,
):
    at = place()
    xl, mp = at["xl"], at["y"] * 2 + at["xl"]
    dp = at["xh"] * 8 + at["z"] * 2 + at["c"]
    everyone = dp * 8 + mp
    depth, half = g_wz.shape
    model = hid.shape[2]
    own_heads = g_al.shape[1]
    gain_in = wide(small, IN_GAIN, model // 128)
    for s in range(hid.shape[0]):
        h = hid[s].astype(F32)
        mixed[s] = (h + got[s].astype(F32)).astype(BF16)
        inv = lax.rsqrt(jnp.mean(h * h, -1, keepdims=True) + EPS)
        hat = back[s].astype(F32) * gain_in
        g_hid[s] = (
            cot[s].astype(F32) + inv * hat - h * ((inv * inv * inv) * jnp.mean(hat * h, -1, keepdims=True))
        )
    g_wz[...] = gzo[:, 0:half]
    g_wo[...] = gzo[:, half : 2 * half]
    g_wx[...] = gxe[:, 0:half]
    g_wdt[...] = gxe[:, half : half + 128].T[0:own_heads]

    def cut(values, start, count):
        width = values.shape[1]
        return pltpu.roll(values, lax.rem(width - start, width), 1)[:, 0:count]

    pairs = half // 64
    own = cut(bcs[0, depth : depth + 8] + bcs[1, depth : depth + 8], mp * g_gain.shape[1], g_gain.shape[1])
    g_gain[...] = own[0:1] / gain[...].astype(F32)
    rows = jnp.concatenate([wide(sums, X_TAPS + t * pairs, pairs) for t in range(7)] + [jnp.zeros((1, 2 * half), F32)], 0)
    own = cut(rows, xl * half + dp * g_kx.shape[1], g_kx.shape[1])
    g_kx[...] = own[0:4]
    g_kxb[...] = own[4:5]
    g_og[...] = own[5:6]
    per_head = head_sums(rows, head_pick(2 * half))
    g_ds[...] = cut(per_head, xl * own_heads, own_heads)[6:7]
    per_head = jnp.concatenate([sums[64:72]], 0)
    per_head = cut(per_head, xl * own_heads, own_heads)
    first = X_TAPS + 7 * pairs - 64
    g_al[...] = per_head[first : first + 1]
    g_db[...] = per_head[first + 1 : first + 2]
    rows = jnp.concatenate([wide(sums, BC_TAPS + 2 * t, 2) for t in range(5)] + [jnp.zeros((3, 256), F32)], 0)
    own = cut(rows, everyone * 2, 128)
    g_kbc[...] = jnp.concatenate([own, jnp.zeros((120, 128), F32)], 0).T[0:2, 0:4]
    g_kbcb[...] = own[4:5, 0:2]
    total = jnp.concatenate([bcs[0, 0:depth], bcs[1, 0:depth]], 1)
    g_wbc[...] = pltpu.roll(total, lax.rem(depth - mp * 12, depth), 0)[0:12]


def finish_call(hidden, cotangent, got, back, small, gain, gzo, gxe, sums, bcs, own_heads):
    depth, half = gzo.shape[0], gzo.shape[1] // 2
    shapes = [
        (hidden.shape, BF16), (hidden.shape, F32), ((1, hidden.shape[2] // 128), F32), ((depth, half), F32),
        ((depth, half), F32), ((own_heads, depth), F32), ((12, 256), F32), ((4, half // 16), F32),
        ((1, half // 16), F32), ((2, 4), F32), ((1, 2), F32), ((1, own_heads), F32), ((1, own_heads), F32),
        ((1, own_heads), F32), ((1, half // 16), F32), ((depth, half), F32),
    ]
    return pl.pallas_call(
        finish_kernel,
        in_specs=[IN_VMEM] * 10,
        out_specs=[IN_VMEM] * len(shapes),
        out_shape=[like(*shape) for shape in shapes],
        name="finish",
        compiler_params=pltpu.CompilerParams(vmem_limit_bytes=VMEM_LIMIT),
    )(hidden, cotangent, got, back, small, gain, gzo, gxe, sums, bcs)


def local(
    hidden, segments, cotangent, norm_gain, w_z, w_x, w_dt, w_bc, conv_x, conv_x_bias, conv_bc, conv_bc_bias,
    a_log, d_skip, dt_bias, out_gain, w_out,
):
    _, _, model = hidden.shape
    depth, half = w_z.shape
    width = 2 * half
    own_heads = a_log.shape[0]
    lay = Layout(width)

    small_args = [
        norm_gain[None], conv_x, conv_x_bias[None], conv_bc.T, conv_bc_bias[None], out_gain[None],
        a_log[None], d_skip[None], dt_bias[None],
    ]
    w2 = jnp.stack([w_z, w_out.T])
    zx, xin, bcin, dt, bcc, y_out, starts, gon, normed, cot_all, w2_all, wxe_all, stat, small, tok = forward_call(
        hidden, cotangent, w2, segments, w_x, w_dt.T, w_bc, small_args
    )
    full_xe = wxe_all.reshape(model, lay.total)
    got_out, grad_normed, zo_sum, xe_sum, sums, bc_sum = backward_call(
        tok, stat, small, zx, gon, y_out, xin, bcin, dt, bcc, starts, cot_all, normed,
        w2_all.reshape(2, model, width), full_xe,
    )
    (
        mixed, g_hid, g_gain, g_wz, g_wx, g_wdt, g_wbc, g_kx, g_kxb, g_kbc, g_kbcb, g_al, g_ds, g_db, g_og, g_wo,
    ) = finish_call(
        hidden, cotangent, got_out, grad_normed, small, norm_gain[None], zo_sum, xe_sum, sums, bc_sum, own_heads
    )
    return (
        mixed, g_hid, g_gain[0], g_wz, g_wx, g_wdt.T, g_wbc, g_kx, g_kxb[0], g_kbc.T, g_kbcb[0], g_al[0], g_ds[0],
        g_db[0], g_og[0], g_wo.T,
    )


def solution(mesh):
    in_specs = (
        P("dp", "mp", None),
        P("dp", None),
        P("dp", "mp", None),
        P(("dp", "mp")),
        P("dp", "mp"),
        P("dp", "mp"),
        P("dp", "mp"),
        P(("dp", "mp"), None),
        P(None, ("mp", "dp")),
        P(("mp", "dp")),
        P(None, ("dp", "mp")),
        P(("dp", "mp")),
        P("mp"),
        P("mp"),
        P("mp"),
        P(("mp", "dp")),
        P("mp", "dp"),
    )
    out_specs = (
        P("dp", "mp", None),
        P("dp", "mp", None),
        P(("dp", "mp")),
        P("dp", "mp"),
        P("dp", "mp"),
        P("dp", "mp"),
        P(("dp", "mp"), None),
        P(None, ("mp", "dp")),
        P(("mp", "dp")),
        P(None, ("dp", "mp")),
        P(("dp", "mp")),
        P("mp"),
        P("mp"),
        P("mp"),
        P(("mp", "dp")),
        P("mp", "dp"),
    )
    return jax.shard_map(local, mesh=mesh, in_specs=in_specs, out_specs=out_specs, check_vma=False)
```
